256 devices in a mesh: dp: 4 (over x), fsdp: 2 (over core), tp: 32 (over z, y).
Axes of the slice: x: 4, y: 4, z: 8, core: 2. Of those that a mesh axis runs over, the one named last changes fastest.
Arguments:
- momentum: float32 [4, 8192, 8192], P('dp', 'fsdp', 'tp'), may hold values from -90 to 90
- gradient: bfloat16 [4, 8192, 8192], P('dp', 'fsdp', 'tp'), may hold values from -6 to 6
- basis: float32 [8192, 512], P('tp', 'fsdp'), may hold values from -6 to 6
Outputs:
- new_momentum: float32 [4, 8192, 8192], P('dp', 'fsdp', 'tp')
- new_basis: float32 [8192, 512], P('tp', 'fsdp')
- update: bfloat16 [8192, 8192], P('fsdp', 'tp')
The draws below stay inside these ranges and needn't reach their ends.
All inputs are finite; a program needn't handle non-finite values.
Results may differ from the reference program's by a relative error of at most 0.025.
Values may be sent and summed in bfloat16 or wider, within the bound.
A program may use at most 128 MiB of HBM per device.

```python
import jax
import jax.numpy as jnp
from jax import lax

D = 8192
R = 512
N_DP = 4


def draw_momentum(key, part):
    key = jax.random.fold_in(key, 11)
    column = jnp.arange(D, dtype=jnp.float32) / (D - 1)
    column_scale = jnp.exp(column * jnp.log(30.0))
    values = jax.random.truncated_normal(key, -6.0, 6.0, (N_DP, D, D), jnp.float32) * 0.5
    return (values * column_scale[None, None, :]).astype(jnp.float32)


def block_levels(own_key, dims, shards, least, high):
    gain, own = 1.0, jax.random.fold_in(own_key, 6)
    for position, blocks in shards:
        heights = jnp.exp(jax.random.uniform(jax.random.fold_in(own, position), (blocks,), jnp.float32, least / len(shards), high / len(shards)))
        gain = gain * jnp.repeat(heights, dims[position] // blocks).reshape([-1 if axis == position else 1 for axis in range(len(dims))])
    return gain


def gaussian(own_key, extent, scale, most, pieces=(), kind=jnp.bfloat16):
    entries = jax.random.normal(own_key, extent, jnp.float32) * scale
    if len(pieces) > 0:
        entries = block_levels(own_key, extent, pieces, -0.22, 0.18) * entries
    return jnp.clip(entries, min=-most, max=most).astype(kind)


def setup_inputs(seed: int = 0) -> dict:
    arg_keys = jax.random.split(jax.random.key(seed), 4)
    return {
        "momentum": draw_momentum(jax.random.fold_in(arg_keys[3], 71), 0),
        "gradient": gaussian(arg_keys[1], (N_DP, D, D), 1.0, 6.0, ((0, 4), (1, 2), (2, 32))),
        "basis": gaussian(arg_keys[2], (D, R), 1.0, 6.0, ((0, 32), (1, 2)), jnp.float32),
    }


def reference(momentum, gradient, basis):
    basis_low = basis.astype(jnp.bfloat16)

    def left_term(pair):
        buffer_low = (pair[0] + pair[1].astype(jnp.float32)).astype(jnp.bfloat16)
        product = jnp.dot(buffer_low.astype(jnp.float32), basis_low.astype(jnp.float32), preferred_element_type=jnp.float32)
        return lax.optimization_barrier(product.astype(jnp.bfloat16)).astype(jnp.float32)
    left_mean = lax.optimization_barrier(jnp.sum(lax.map(left_term, (momentum, gradient)), axis=0)) / N_DP
    gram = jnp.dot(left_mean.T, left_mean, precision=lax.Precision.HIGHEST)
    lower = jnp.linalg.cholesky(gram)
    inverse = jax.scipy.linalg.solve_triangular(lower, jnp.eye(R, dtype=jnp.float32), lower=True)
    ortho = jnp.dot(left_mean, inverse.T, precision=lax.Precision.HIGHEST)
    ortho_low = ortho.astype(jnp.bfloat16)

    def right_term(pair):
        buffer_low = (pair[0] + pair[1].astype(jnp.float32)).astype(jnp.bfloat16)
        product = lax.dot_general(ortho_low.astype(jnp.float32), buffer_low.astype(jnp.float32), (((0,), (0,)), ((), ())), preferred_element_type=jnp.float32)
        return lax.optimization_barrier(product.astype(jnp.bfloat16)).astype(jnp.float32)
    right_mean = lax.optimization_barrier(jnp.sum(lax.map(right_term, (momentum, gradient)), axis=0)) / N_DP
    right_low = right_mean.astype(jnp.bfloat16)
    lowrank = jnp.dot(ortho_low.astype(jnp.float32), right_low.astype(jnp.float32), preferred_element_type=jnp.float32)

    def feedback(pair):
        return pair[0] + pair[1].astype(jnp.float32) - 0.05 * lowrank
    new_momentum = lax.map(feedback, (momentum, gradient))
    scales = 1.0 / jnp.sqrt(lax.optimization_barrier(jnp.mean(right_mean * right_mean, axis=1)) + 1e-05)
    next_rows = right_mean * scales[:, None]
    new_basis = next_rows.T
    next_low = next_rows.astype(jnp.bfloat16)
    update = (jnp.dot(ortho_low.astype(jnp.float32), next_low.astype(jnp.float32), preferred_element_type=jnp.float32) * (D / jnp.sqrt(jnp.float32(R)))).astype(jnp.bfloat16)
    return (new_momentum, new_basis, update)
```

```python
import functools

import jax
import jax.numpy as jnp
from jax import lax
from jax.experimental import pallas as pl
from jax.experimental.pallas import tpu as pltpu
from jax.sharding import PartitionSpec as P

D = 8192
R = 512
NX, NY, NZ = 4, 4, 8
ROWS = 32
LOCAL_ROWS = NX * NY * NZ * ROWS
COLS = 256
MESH = pl.DeviceIdType.MESH
F32, BF16 = jnp.float32, jnp.bfloat16
MIB = 2**20


def place():
    tp = lax.axis_index("tp")
    return lax.axis_index("dp"), lax.axis_index("fsdp"), lax.rem(tp, NY), lax.div(tp, NY)


def x_peer(d):
    p = lax.rem(lax.axis_index("dp") + d, NX)
    return p, {"dp": p}


def y_peer(d):
    _, _, y, z = place()
    p = lax.rem(y + d, NY)
    return p, {"tp": z * NY + p}


def z_peer(d):
    _, _, y, z = place()
    p = lax.rem(z + d, NZ)
    return p, {"tp": p * NY + y}


def pair_peer(d):
    x, c, _, _ = place()
    p = lax.rem(x * 2 + c + d, 2 * NX)
    return p, {"dp": lax.div(p, 2), "fsdp": lax.rem(p, 2)}


SPANS = {"x": (x_peer, NX), "y": (y_peer, NY), "z": (z_peer, NZ), "pair": (pair_peer, 2 * NX)}


def peers(axis):
    find, n = SPANS[axis]
    return [find(d) for d in range(1, n)]


def greet(devices):
    barrier = pltpu.get_barrier_semaphore()
    for device in devices:
        pl.semaphore_signal(barrier, inc=1, device_id=device, device_id_type=MESH)
    pl.semaphore_wait(barrier, len(devices))


class Sender:
    def __init__(self, send, recv):
        self.send, self.recv, self.used = send, recv, 0

    def start(self, src, dst, device):
        k = self.used
        self.used += 1
        copy = pltpu.make_async_remote_copy(
            src_ref=src,
            dst_ref=dst,
            send_sem=self.send.at[k],
            recv_sem=self.recv.at[k],
            device_id=device,
            device_id_type=MESH,
        )
        copy.start()
        return copy


def settle(copies):
    for copy in copies:
        copy.wait()


def front_kernel(
    mom, grad, basis, left, gram, right,
    low, base, part, rx1, ry1, rz1, sx1, sy1, sz1, rx2, ry2, rz2, sx2, sy2, sz2, rx3, ry3, rz3,
    gsend, grecv, tpart, trecv, tsum, send, recv,
):
    x, c, y, z = place()
    sender = Sender(send, recv)
    sibling = {"fsdp": 1 - c}
    every = [p for a in ("x", "y", "z", "pair") for _, p in peers(a)]
    greet(every)

    base[c] = basis[...].astype(BF16)
    basis_copy = sender.start(base.at[c], base.at[c], sibling)

    def lower(i, _):
        rows = pl.ds(pl.multiple_of(i * 256, 256), 256)
        low[rows, :] = (mom[0, rows, :] + grad[0, rows, :].astype(F32)).astype(BF16)
        return 0

    lax.fori_loop(0, LOCAL_ROWS // 256, lower, 0)
    basis_copy.wait()

    def product(i, _):
        rows = pl.ds(pl.multiple_of(i * 256, 256), 256)
        block = low[rows, :]
        xi, yi = lax.div(i, NY), lax.rem(i, NY)
        for h in range(2):
            value = jnp.dot(block, base[h], preferred_element_type=F32).astype(BF16)
            part[xi, yi, :, :, h * 256 : (h + 1) * 256] = value.reshape(NZ, ROWS, 256)
        return 0

    lax.fori_loop(0, NX * NY, product, 0)

    cx, cy, cz = pl.ds(0, 256), pl.ds(256, 128), pl.ds(384, 128)
    px, py, pz = peers("x"), peers("y"), peers("z")

    x1 = [sender.start(part.at[p, :, :, :, cx], rx1.at[k], dev) for k, (p, dev) in enumerate(px)]
    y1 = [sender.start(part.at[:, p, :, :, cy], ry1.at[k], dev) for k, (p, dev) in enumerate(py)]
    z1 = [sender.start(part.at[:, :, p, :, cz], rz1.at[k], dev) for k, (p, dev) in enumerate(pz)]
    settle(x1)
    for i in range(NY):
        total = part[x, i, :, :, 0:256].astype(F32)
        for k in range(NX - 1):
            total = total + rx1[k, i].astype(F32)
        sx1[i] = total.astype(BF16)
    x2 = [sender.start(sx1.at[p], rx2.at[k], dev) for k, (p, dev) in enumerate(py)]
    settle(y1)
    for i in range(NX):
        total = part[i, y, :, :, 256:384].astype(F32)
        for k in range(NY - 1):
            total = total + ry1[k, i].astype(F32)
        sy1[i] = total.astype(BF16)
    y2 = [sender.start(sy1.at[p], ry2.at[k], dev) for k, (p, dev) in enumerate(px)]
    settle(z1)
    for i in range(NX):
        total = part[i, :, z, :, 384:512].astype(F32)
        for k in range(NZ - 1):
            total = total + rz1[k, i].astype(F32)
        sz1[i] = total.astype(BF16)
    z2 = [sender.start(sz1.at[p], rz2.at[k], dev) for k, (p, dev) in enumerate(px)]

    settle(x2)
    total = sx1[y].astype(F32)
    for k in range(NY - 1):
        total = total + rx2[k].astype(F32)
    sx2[...] = total.astype(BF16)
    x3 = [sender.start(sx2.at[p], rx3.at[k], dev) for k, (p, dev) in enumerate(pz)]
    settle(y2)
    total = sy1[x].astype(F32)
    for k in range(NX - 1):
        total = total + ry2[k].astype(F32)
    sy2[...] = total.astype(BF16)
    y3 = [sender.start(sy2.at[p], ry3.at[k], dev) for k, (p, dev) in enumerate(pz)]
    settle(z2)
    total = sz1[x].astype(F32)
    for k in range(NX - 1):
        total = total + rz2[k].astype(F32)
    sz2[...] = total.astype(BF16)
    z3 = [sender.start(sz2.at[p], rz3.at[k], dev) for k, (p, dev) in enumerate(py)]

    settle(x3)
    total = sx2[z].astype(F32)
    for k in range(NZ - 1):
        total = total + rx3[k].astype(F32)
    left[x, y, z, :, 0:256] = (total / NX).astype(BF16)
    mine = left.at[x, y, z, :, cx]
    x4 = [sender.start(mine, mine, dev) for _, dev in pz]
    settle(y3)
    total = sy2[z].astype(F32)
    for k in range(NZ - 1):
        total = total + ry3[k].astype(F32)
    left[x, y, z, :, 256:384] = (total / NX).astype(BF16)
    mine = left.at[x, y, z, :, cy]
    y4 = [sender.start(mine, mine, dev) for _, dev in pz]
    settle(z3)
    total = sz2[y].astype(F32)
    for k in range(NY - 1):
        total = total + rz3[k].astype(F32)
    left[x, y, z, :, 384:512] = (total / NX).astype(BF16)
    mine = left.at[x, y, z, :, cz]
    z4 = [sender.start(mine, mine, dev) for _, dev in py]

    settle(x4)
    mine = left.at[x, y, :, :, cx]
    x5 = [sender.start(mine, mine, dev) for _, dev in py]
    settle(y4)
    mine = left.at[x, y, :, :, cy]
    y5 = [sender.start(mine, mine, dev) for _, dev in px]
    settle(z4)
    mine = left.at[x, :, z, :, cz]
    z5 = [sender.start(mine, mine, dev) for _, dev in px]

    settle(x5)
    mine = left.at[x, :, :, :, cx]
    x6 = [sender.start(mine, mine, dev) for _, dev in px]
    settle(y5)
    mine = left.at[:, y, :, :, cy]
    y6 = [sender.start(mine, mine, dev) for _, dev in py]
    settle(z5)
    mine = left.at[:, :, z, :, cz]
    z6 = [sender.start(mine, mine, dev) for _, dev in pz]
    settle(x6 + y6 + z6)

    gsend[...] = jnp.zeros_like(gsend)
    tpart[...] = jnp.zeros_like(tpart)

    def products(i, _):
        xi, half = lax.div(i, 2), lax.rem(i, 2)
        block = left[xi, pl.ds(half * 2, 2)].reshape(512, R)
        rows = pl.ds(pl.multiple_of(i * 512, 512), 512)
        gsend[...] += lax.dot_general(
            block, block, (((0,), (0,)), ((), ())), preferred_element_type=F32
        )
        tpart[...] += lax.dot_general(
            low[rows, :], block, (((0,), (0,)), ((), ())), preferred_element_type=F32
        ).reshape(tpart.shape)
        return 0

    lax.fori_loop(0, 8, products, 0)
    g1 = sender.start(gsend, grecv, sibling)
    around = peers("pair")
    t1 = [sender.start(tpart.at[p], trecv.at[k], dev) for k, (p, dev) in enumerate(around)]
    settle(t1)
    me = x * 2 + c
    total = tpart[me]
    for k in range(2 * NX - 1):
        total = total + trecv[k]
    right[me] = total / NX
    mine = right.at[me]
    t2 = [sender.start(mine, mine, dev) for _, dev in around]
    g1.wait()
    gram[...] = gsend[...] + grecv[...]
    settle(t2)


def front(momentum, gradient, basis):
    vmem = pl.BlockSpec(memory_space=pltpu.VMEM)
    scratch = [
        pltpu.VMEM((LOCAL_ROWS, COLS), BF16),
        pltpu.VMEM((2, COLS, 256), BF16),
        pltpu.VMEM((NX, NY, NZ, ROWS, R), BF16),
        pltpu.VMEM((3, NY, NZ, ROWS, 256), BF16),
        pltpu.VMEM((3, NX, NZ, ROWS, 128), BF16),
        pltpu.VMEM((7, NX, NY, ROWS, 128), BF16),
        pltpu.VMEM((NY, NZ, ROWS, 256), BF16),
        pltpu.VMEM((NX, NZ, ROWS, 128), BF16),
        pltpu.VMEM((NX, NY, ROWS, 128), BF16),
        pltpu.VMEM((3, NZ, ROWS, 256), BF16),
        pltpu.VMEM((3, NZ, ROWS, 128), BF16),
        pltpu.VMEM((3, NY, ROWS, 128), BF16),
        pltpu.VMEM((NZ, ROWS, 256), BF16),
        pltpu.VMEM((NZ, ROWS, 128), BF16),
        pltpu.VMEM((NY, ROWS, 128), BF16),
        pltpu.VMEM((7, ROWS, 256), BF16),
        pltpu.VMEM((7, ROWS, 128), BF16),
        pltpu.VMEM((3, ROWS, 128), BF16),
        pltpu.VMEM((R, R), F32),
        pltpu.VMEM((R, R), F32),
        pltpu.VMEM((8, 32, R), F32),
        pltpu.VMEM((7, 32, R), F32),
        pltpu.VMEM((32, R), F32),
        pltpu.SemaphoreType.DMA((104,)),
        pltpu.SemaphoreType.DMA((104,)),
    ]
    return pl.pallas_call(
        front_kernel,
        out_shape=(
            jax.ShapeDtypeStruct((NX, NY, NZ, ROWS, R), BF16),
            jax.ShapeDtypeStruct((R, R), F32),
            jax.ShapeDtypeStruct((8, 32, R), F32),
        ),
        in_specs=[vmem] * 3,
        out_specs=(vmem,) * 3,
        scratch_shapes=scratch,
        compiler_params=pltpu.CompilerParams(
            collective_id=0, has_side_effects=True, vmem_limit_bytes=56 * MIB
        ),
        name="front",
    )(momentum, gradient, basis)


def squares_kernel(right, total, own, ry, mid, rz, send, recv):
    sender = Sender(send, recv)
    py, pz = peers("y"), peers("z")
    greet([dev for _, dev in py + pz])
    values = right[...]
    own[...] = jnp.broadcast_to(jnp.sum(values * values, axis=0, keepdims=True), own.shape)
    y1 = [sender.start(own, ry.at[k], dev) for k, (_, dev) in enumerate(py)]
    settle(y1)
    value = own[...]
    for k in range(NY - 1):
        value = value + ry[k]
    mid[...] = value
    z1 = [sender.start(mid, rz.at[k], dev) for k, (_, dev) in enumerate(pz)]
    settle(z1)
    value = mid[...]
    for k in range(NZ - 1):
        value = value + rz[k]
    total[...] = value


def squares_of(right):
    vmem = pl.BlockSpec(memory_space=pltpu.VMEM)
    return pl.pallas_call(
        squares_kernel,
        out_shape=jax.ShapeDtypeStruct((8, R), F32),
        in_specs=[vmem],
        out_specs=vmem,
        scratch_shapes=[
            pltpu.VMEM((8, R), F32),
            pltpu.VMEM((3, 8, R), F32),
            pltpu.VMEM((8, R), F32),
            pltpu.VMEM((7, 8, R), F32),
            pltpu.SemaphoreType.DMA((10,)),
            pltpu.SemaphoreType.DMA((10,)),
        ],
        compiler_params=pltpu.CompilerParams(collective_id=1, has_side_effects=True),
        name="squares",
    )(right)


def finish_kernel(left, high, rest, right, following, mom, grad, new_mom, update):
    block = left[...]
    ortho = (
        jnp.dot(block, high[...], preferred_element_type=F32)
        + jnp.dot(block, rest[...], preferred_element_type=F32)
    ).astype(BF16)
    across = (((1,), (1,)), ((), ()))
    lowrank = lax.dot_general(ortho, right[...], across, preferred_element_type=F32)
    new_mom[0] = mom[0] + grad[0].astype(F32) - 0.05 * lowrank
    factor = D / (R**0.5)
    product = lax.dot_general(ortho, following[...], across, preferred_element_type=F32)
    update[...] = (product * factor).astype(BF16)


def finish(left, high, rest, right, following, momentum, gradient):
    tile = 512
    whole = lambda shape: pl.BlockSpec(shape, lambda i: (0,) * len(shape))
    rows = pl.BlockSpec((tile, R), lambda i: (i, 0))
    cube = pl.BlockSpec((1, tile, COLS), lambda i: (0, i, 0))
    return pl.pallas_call(
        finish_kernel,
        grid=(LOCAL_ROWS // tile,),
        out_shape=(
            jax.ShapeDtypeStruct((1, LOCAL_ROWS, COLS), F32),
            jax.ShapeDtypeStruct((LOCAL_ROWS, COLS), BF16),
        ),
        in_specs=[rows, whole((R, R)), whole((R, R)), whole((COLS, R)), whole((COLS, R)), cube, cube],
        out_specs=(cube, pl.BlockSpec((tile, COLS), lambda i: (i, 0))),
        compiler_params=pltpu.CompilerParams(vmem_limit_bytes=40 * MIB),
        name="finish",
    )(left, high, rest, right, following, momentum, gradient)


def inverse_transposed(gram):
    lower = jnp.linalg.cholesky(gram)
    inverse = jax.scipy.linalg.solve_triangular(lower, jnp.eye(R, dtype=F32), lower=True)
    return inverse.T


def shards(momentum, gradient, basis):
    left, gram, right = front(momentum, gradient, basis)
    upper = inverse_transposed(gram)
    right_mean = jnp.dot(right.reshape(COLS, R), upper, precision=lax.Precision.HIGHEST)
    squares = squares_of(right_mean)[0:1]
    following = right_mean * (1.0 / jnp.sqrt(squares / D + 1e-05))
    new_basis = lax.dynamic_slice_in_dim(following, lax.axis_index("fsdp") * 256, 256, 1)
    high = upper.astype(BF16)
    rest = (upper - high.astype(F32)).astype(BF16)
    new_momentum, update = finish(
        left.reshape(LOCAL_ROWS, R), high, rest, right_mean.astype(BF16),
        following.astype(BF16), momentum, gradient,
    )
    return (new_momentum, new_basis, update)


def solution(mesh):
    in_specs = (P("dp", "fsdp", "tp"), P("dp", "fsdp", "tp"), P("tp", "fsdp"))
    out_specs = (P("dp", "fsdp", "tp"), P("tp", "fsdp"), P("fsdp", "tp"))
    return jax.shard_map(shards, mesh=mesh, in_specs=in_specs, out_specs=out_specs, check_vma=False)
```

```python
import jax
import jax.numpy as jnp
from jax import lax
from jax.experimental import pallas as pl
from jax.experimental.pallas import tpu as pltpu
from jax.sharding import PartitionSpec as P

D = 8192
R = 512
NX, NY, NZ = 4, 4, 8
ROWS = 32
LOCAL_ROWS = NX * NY * NZ * ROWS
COLS = 256
MESH = pl.DeviceIdType.MESH
F32, BF16 = jnp.float32, jnp.bfloat16
HIGH = lax.Precision.HIGHEST
MIB = 2**20


def place():
    tp = lax.axis_index("tp")
    return lax.axis_index("dp"), lax.axis_index("fsdp"), lax.rem(tp, NY), lax.div(tp, NY)


def x_peer(d):
    p = lax.rem(lax.axis_index("dp") + d, NX)
    return p, {"dp": p}


def y_peer(d):
    _, _, y, z = place()
    p = lax.rem(y + d, NY)
    return p, {"tp": z * NY + p}


def z_peer(d):
    _, _, y, z = place()
    p = lax.rem(z + d, NZ)
    return p, {"tp": p * NY + y}


def pair_peer(d):
    x, c, _, _ = place()
    p = lax.rem(x * 2 + c + d, 2 * NX)
    return p, {"dp": lax.div(p, 2), "fsdp": lax.rem(p, 2)}


SPANS = {"x": (x_peer, NX), "y": (y_peer, NY), "z": (z_peer, NZ), "pair": (pair_peer, 2 * NX)}


def peers(axis):
    find, n = SPANS[axis]
    return [find(d) for d in range(1, n)]


def greet(devices):
    barrier = pltpu.get_barrier_semaphore()
    for device in devices:
        pl.semaphore_signal(barrier, inc=1, device_id=device, device_id_type=MESH)
    pl.semaphore_wait(barrier, len(devices))


class Sender:
    def __init__(self, send, recv):
        self.send, self.recv, self.used = send, recv, 0

    def make(self, src, dst, device):
        k = self.used
        self.used += 1
        return pltpu.make_async_remote_copy(
            src_ref=src,
            dst_ref=dst,
            send_sem=self.send.at[k],
            recv_sem=self.recv.at[k],
            device_id=device,
            device_id_type=MESH,
        )

    def start(self, src, dst, device):
        copy = self.make(src, dst, device)
        copy.start()
        return copy


def settle(copies):
    for copy in copies:
        copy.wait()


def splat_rows(v, i):
    return jnp.broadcast_to(v[i:i+1,:], (8,128))

def diag_inverse(load):
    n=16
    sub=lax.broadcasted_iota(jnp.int32,(8,128),0)
    lane=lax.broadcasted_iota(jnp.int32,(8,128),1)
    G=[load(g) for g in range(n)]
    Y=[(lane==sub+8*g).astype(F32) for g in range(n)]
    out=[]
    for p in range(n):
        at=8*p
        C=[jnp.broadcast_to(G[p][:,at+k:at+k+1],(8,128)) for k in range(8)]
        c={(i,k): splat_rows(C[k],i) for k in range(8) for i in range(k,8)}
        r=[None]*8; l={}
        for j in range(8):
            piv=c[j,j]
            rr=lax.rsqrt(piv)
            rr=rr*(1.5-0.5*piv*rr*rr)
            r[j]=rr
            for i in range(j+1,8): l[i,j]=c[i,j]*rr
            for k in range(j+1,8):
                for i in range(k,8):
                    c[i,k]=c[i,k]-l[i,j]*l[k,j]
        us,ys=[],[]
        g0,y0=G[p],Y[p]
        done_y=jnp.zeros((8,128),F32)
        Lc=[]
        for j in range(8):
            col=C[j]
            for i in range(j): col=col-Lc[i]*l[j,i]
            col=col*r[j]
            Lc.append(col)
            u=splat_rows(g0,j)*r[j]
            yv=splat_rows(y0,j)*r[j]
            us.append(u); ys.append(yv)
            m=jnp.where(sub>j,col,0.0)
            g0=g0-m*u
            y0=y0-m*yv
            done_y=jnp.where(sub==j,yv,done_y)
        out.append(done_y)
        for g in range(p+1,n):
            Cg=[jnp.broadcast_to(G[g][:,at+k:at+k+1],(8,128)) for k in range(8)]
            L=[]
            gg,yy=G[g],Y[g]
            for j in range(8):
                col=Cg[j]
                for i in range(j): col=col-L[i]*l[j,i]
                col=col*r[j]; L.append(col)
                gg=gg-col*us[j]
                yy=yy-col*ys[j]
            G[g],Y[g]=gg,yy
    return out

def nt(a, b, precision=HIGH):
    return lax.dot_general(
        a, b, (((1,), (1,)), ((), ())), precision=precision, preferred_element_type=F32
    )


def nn(a, b):
    return jnp.dot(a, b, precision=HIGH, preferred_element_type=F32)

def inverse_factor(a, out, between):
    out[...] = jnp.zeros_like(out)

    def step(kb, _):
        between(kb)
        base = pl.multiple_of(kb * 128, 128)
        rows = diag_inverse(lambda g: a[pl.ds(base + 8 * g, 8), pl.ds(base, 128)])
        for g in range(16):
            out[pl.ds(base + 8 * g, 8), pl.ds(base, 128)] = rows[g]
        for s in range(4):

            @pl.when(kb == s)
            def _():
                lo, hi = s * 128, (s + 1) * 128
                block = out[lo:hi, lo:hi]
                if s > 0:
                    out[lo:hi, 0:lo] = nn(block, out[lo:hi, 0:lo])
                if s < 3:
                    panel = nt(a[hi:R, lo:hi], block)
                    a[hi:R, hi:R] = a[hi:R, hi:R] - nt(panel, panel)
                    out[hi:R, 0:hi] = out[hi:R, 0:hi] - nn(panel, out[lo:hi, 0:hi])

        return 0

    lax.fori_loop(0, 4, step, 0)


def front_kernel(
    mom, grad, basis, left, right_low, next_low, new_basis,
    low, base, part, rx1, ry1, rz1, sx1, sy1, sz1, rx2, ry2, rz2, sx2, sy2, sz2, rx3, ry3, rz3,
    gsend, grecv, tpart, trecv, right, inverse, following, own, ry, mid, rz, send, recv,
):
    x, c, y, z = place()
    sender = Sender(send, recv)
    sibling = {"fsdp": 1 - c}
    every = [p for a in ("x", "y", "z", "pair") for _, p in peers(a)]
    greet(every)

    base[c] = basis[...].astype(BF16)
    basis_copy = sender.start(base.at[c], base.at[c], sibling)

    def lower(i, _):
        rows = pl.ds(pl.multiple_of(i * 256, 256), 256)
        low[rows, :] = (mom[0, rows, :] + grad[0, rows, :].astype(F32)).astype(BF16)
        return 0

    lax.fori_loop(0, LOCAL_ROWS // 256, lower, 0)
    basis_copy.wait()

    def product(i, _):
        rows = pl.ds(pl.multiple_of(i * 256, 256), 256)
        block = low[rows, :]
        xi, yi = lax.div(i, NY), lax.rem(i, NY)
        for h in range(2):
            value = jnp.dot(block, base[h], preferred_element_type=F32).astype(BF16)
            part[xi, yi, :, :, h * 256 : (h + 1) * 256] = value.reshape(NZ, ROWS, 256)
        return 0

    lax.fori_loop(0, NX * NY, product, 0)

    cx, cy, cz = pl.ds(0, 256), pl.ds(256, 128), pl.ds(384, 128)
    px, py, pz = peers("x"), peers("y"), peers("z")

    x1 = [sender.start(part.at[p, :, :, :, cx], rx1.at[k], dev) for k, (p, dev) in enumerate(px)]
    y1 = [sender.start(part.at[:, p, :, :, cy], ry1.at[k], dev) for k, (p, dev) in enumerate(py)]
    z1 = [sender.start(part.at[:, :, p, :, cz], rz1.at[k], dev) for k, (p, dev) in enumerate(pz)]
    settle(x1)
    for i in range(NY):
        total = part[x, i, :, :, 0:256].astype(F32)
        for k in range(NX - 1):
            total = total + rx1[k, i].astype(F32)
        sx1[i] = total.astype(BF16)
    x2 = [sender.start(sx1.at[p], rx2.at[k], dev) for k, (p, dev) in enumerate(py)]
    settle(y1)
    for i in range(NX):
        total = part[i, y, :, :, 256:384].astype(F32)
        for k in range(NY - 1):
            total = total + ry1[k, i].astype(F32)
        sy1[i] = total.astype(BF16)
    y2 = [sender.start(sy1.at[p], ry2.at[k], dev) for k, (p, dev) in enumerate(px)]
    settle(z1)
    for i in range(NX):
        total = part[i, :, z, :, 384:512].astype(F32)
        for k in range(NZ - 1):
            total = total + rz1[k, i].astype(F32)
        sz1[i] = total.astype(BF16)
    z2 = [sender.start(sz1.at[p], rz2.at[k], dev) for k, (p, dev) in enumerate(px)]

    settle(x2)
    total = sx1[y].astype(F32)
    for k in range(NY - 1):
        total = total + rx2[k].astype(F32)
    sx2[...] = total.astype(BF16)
    x3 = [sender.start(sx2.at[p], rx3.at[k], dev) for k, (p, dev) in enumerate(pz)]
    settle(y2)
    total = sy1[x].astype(F32)
    for k in range(NX - 1):
        total = total + ry2[k].astype(F32)
    sy2[...] = total.astype(BF16)
    y3 = [sender.start(sy2.at[p], ry3.at[k], dev) for k, (p, dev) in enumerate(pz)]
    settle(z2)
    total = sz1[x].astype(F32)
    for k in range(NX - 1):
        total = total + rz2[k].astype(F32)
    sz2[...] = total.astype(BF16)
    z3 = [sender.start(sz2.at[p], rz3.at[k], dev) for k, (p, dev) in enumerate(py)]

    settle(x3)
    total = sx2[z].astype(F32)
    for k in range(NZ - 1):
        total = total + rx3[k].astype(F32)
    left[x, y, z, :, 0:256] = (total / NX).astype(BF16)
    mine = left.at[x, y, z, :, cx]
    x4 = [sender.start(mine, mine, dev) for _, dev in pz]
    settle(y3)
    total = sy2[z].astype(F32)
    for k in range(NZ - 1):
        total = total + ry3[k].astype(F32)
    left[x, y, z, :, 256:384] = (total / NX).astype(BF16)
    mine = left.at[x, y, z, :, cy]
    y4 = [sender.start(mine, mine, dev) for _, dev in pz]
    settle(z3)
    total = sz2[y].astype(F32)
    for k in range(NY - 1):
        total = total + rz3[k].astype(F32)
    left[x, y, z, :, 384:512] = (total / NX).astype(BF16)
    mine = left.at[x, y, z, :, cz]
    z4 = [sender.start(mine, mine, dev) for _, dev in py]

    settle(x4)
    mine = left.at[x, y, :, :, cx]
    x5 = [sender.start(mine, mine, dev) for _, dev in py]
    settle(y4)
    mine = left.at[x, y, :, :, cy]
    y5 = [sender.start(mine, mine, dev) for _, dev in px]
    settle(z4)
    mine = left.at[x, :, z, :, cz]
    z5 = [sender.start(mine, mine, dev) for _, dev in px]

    settle(x5)
    mine = left.at[x, :, :, :, cx]
    x6 = [sender.start(mine, mine, dev) for _, dev in px]
    settle(y5)
    mine = left.at[:, y, :, :, cy]
    y6 = [sender.start(mine, mine, dev) for _, dev in py]
    settle(z5)
    mine = left.at[:, :, z, :, cz]
    z6 = [sender.start(mine, mine, dev) for _, dev in pz]
    settle(x6 + y6 + z6)

    gsend[...] = jnp.zeros_like(gsend)
    tpart[...] = jnp.zeros_like(tpart)

    def products(i, _):
        xi, half = lax.div(i, 2), lax.rem(i, 2)
        block = left[xi, pl.ds(half * 2, 2)].reshape(512, R)
        rows = pl.ds(pl.multiple_of(i * 512, 512), 512)
        gsend[...] += lax.dot_general(
            block, block, (((0,), (0,)), ((), ())), preferred_element_type=F32
        )
        tpart[...] += lax.dot_general(
            low[rows, :], block, (((0,), (0,)), ((), ())), preferred_element_type=F32
        ).reshape(tpart.shape)
        return 0

    lax.fori_loop(0, 8, products, 0)
    g1 = sender.start(gsend, grecv, sibling)
    around = peers("pair")
    t1 = [sender.start(tpart.at[p], trecv.at[k], dev) for k, (p, dev) in enumerate(around)]
    me = x * 2 + c
    mine = right.at[me]
    t2 = [sender.make(mine, mine, dev) for _, dev in around]
    g1.wait()
    gsend[...] = gsend[...] + grecv[...]

    def between(kb):
        @pl.when(kb == 2)
        def _():
            settle(t1)
            total = tpart[me]
            for k in range(2 * NX - 1):
                total = total + trecv[k]
            right[me] = total / NX
            for copy in t2:
                copy.start()

    inverse_factor(gsend, inverse, between)
    grecv[...] = inverse[...] - inverse[...].astype(BF16).astype(F32)
    settle(t2)

    mean = nt(right[...].reshape(COLS, R), inverse[...])
    right_low[...] = mean.astype(BF16)
    following[...] = mean
    own[...] = jnp.broadcast_to(jnp.sum(mean * mean, axis=0, keepdims=True), own.shape)
    y7 = [sender.start(own, ry.at[k], dev) for k, (_, dev) in enumerate(py)]

    def ortho(i, _):
        xi, yi = lax.div(i, NY), lax.rem(i, NY)
        block = left[xi, yi].reshape(NZ * ROWS, R)
        high = inverse[...].astype(BF16)
        rest = grecv[...].astype(BF16)
        value = nt(block, high, None) + nt(block, rest, None)
        left[xi, yi] = value.astype(BF16).reshape(NZ, ROWS, R)
        return 0

    lax.fori_loop(0, NX * NY // 2, ortho, 0)
    settle(y7)
    value = own[...]
    for k in range(NY - 1):
        value = value + ry[k]
    mid[...] = value
    z7 = [sender.start(mid, rz.at[k], dev) for k, (_, dev) in enumerate(pz)]
    lax.fori_loop(NX * NY // 2, NX * NY, ortho, 0)
    settle(z7)
    value = mid[...]
    for k in range(NZ - 1):
        value = value + rz[k]
    scale = 1.0 / jnp.sqrt(value[0:1] / D + 1e-05)
    following[...] = following[...] * scale
    next_low[...] = following[...].astype(BF16)
    for core in range(2):

        @pl.when(c == core)
        def _():
            new_basis[...] = following[:, core * 256 : (core + 1) * 256]


def front(momentum, gradient, basis):
    vmem = pl.BlockSpec(memory_space=pltpu.VMEM)
    scratch = [
        pltpu.VMEM((LOCAL_ROWS, COLS), BF16),
        pltpu.VMEM((2, COLS, 256), BF16),
        pltpu.VMEM((NX, NY, NZ, ROWS, R), BF16),
        pltpu.VMEM((3, NY, NZ, ROWS, 256), BF16),
        pltpu.VMEM((3, NX, NZ, ROWS, 128), BF16),
        pltpu.VMEM((7, NX, NY, ROWS, 128), BF16),
        pltpu.VMEM((NY, NZ, ROWS, 256), BF16),
        pltpu.VMEM((NX, NZ, ROWS, 128), BF16),
        pltpu.VMEM((NX, NY, ROWS, 128), BF16),
        pltpu.VMEM((3, NZ, ROWS, 256), BF16),
        pltpu.VMEM((3, NZ, ROWS, 128), BF16),
        pltpu.VMEM((3, NY, ROWS, 128), BF16),
        pltpu.VMEM((NZ, ROWS, 256), BF16),
        pltpu.VMEM((NZ, ROWS, 128), BF16),
        pltpu.VMEM((NY, ROWS, 128), BF16),
        pltpu.VMEM((7, ROWS, 256), BF16),
        pltpu.VMEM((7, ROWS, 128), BF16),
        pltpu.VMEM((3, ROWS, 128), BF16),
        pltpu.VMEM((R, R), F32),
        pltpu.VMEM((R, R), F32),
        pltpu.VMEM((8, 32, R), F32),
        pltpu.VMEM((7, 32, R), F32),
        pltpu.VMEM((8, 32, R), F32),
        pltpu.VMEM((R, R), F32),
        pltpu.VMEM((COLS, R), F32),
        pltpu.VMEM((8, R), F32),
        pltpu.VMEM((3, 8, R), F32),
        pltpu.VMEM((8, R), F32),
        pltpu.VMEM((7, 8, R), F32),
        pltpu.SemaphoreType.DMA((112,)),
        pltpu.SemaphoreType.DMA((112,)),
    ]
    return pl.pallas_call(
        front_kernel,
        out_shape=(
            jax.ShapeDtypeStruct((NX, NY, NZ, ROWS, R), BF16),
            jax.ShapeDtypeStruct((COLS, R), BF16),
            jax.ShapeDtypeStruct((COLS, R), BF16),
            jax.ShapeDtypeStruct((COLS, 256), F32),
        ),
        in_specs=[vmem] * 3,
        out_specs=(vmem,) * 4,
        scratch_shapes=scratch,
        compiler_params=pltpu.CompilerParams(
            collective_id=0, has_side_effects=True, vmem_limit_bytes=56 * MIB
        ),
        name="front",
    )(momentum, gradient, basis)


def finish_kernel(left, right, following, mom, grad, new_mom, update):
    ortho = left[...]
    across = (((1,), (1,)), ((), ()))
    lowrank = lax.dot_general(ortho, right[...], across, preferred_element_type=F32)
    new_mom[0] = mom[0] + grad[0].astype(F32) - 0.05 * lowrank
    factor = D / (R**0.5)
    product = lax.dot_general(ortho, following[...], across, preferred_element_type=F32)
    update[...] = (product * factor).astype(BF16)


def finish(left, right, following, momentum, gradient):
    tile = 512
    whole = lambda shape: pl.BlockSpec(shape, lambda i: (0,) * len(shape))
    rows = pl.BlockSpec((tile, R), lambda i: (i, 0))
    cube = pl.BlockSpec((1, tile, COLS), lambda i: (0, i, 0))
    return pl.pallas_call(
        finish_kernel,
        grid=(LOCAL_ROWS // tile,),
        out_shape=(
            jax.ShapeDtypeStruct((1, LOCAL_ROWS, COLS), F32),
            jax.ShapeDtypeStruct((LOCAL_ROWS, COLS), BF16),
        ),
        in_specs=[rows, whole((COLS, R)), whole((COLS, R)), cube, cube],
        out_specs=(cube, pl.BlockSpec((tile, COLS), lambda i: (i, 0))),
        compiler_params=pltpu.CompilerParams(vmem_limit_bytes=40 * MIB),
        name="finish",
    )(left, right, following, momentum, gradient)


def shards(momentum, gradient, basis):
    ortho, right, following, new_basis = front(momentum, gradient, basis)
    new_momentum, update = finish(
        ortho.reshape(LOCAL_ROWS, R), right, following, momentum, gradient
    )
    return (new_momentum, new_basis, update)


def solution(mesh):
    in_specs = (P("dp", "fsdp", "tp"), P("dp", "fsdp", "tp"), P("tp", "fsdp"))
    out_specs = (P("dp", "fsdp", "tp"), P("tp", "fsdp"), P("fsdp", "tp"))
    return jax.shard_map(shards, mesh=mesh, in_specs=in_specs, out_specs=out_specs, check_vma=False)
```

```python
import jax
import jax.numpy as jnp
from jax import lax
from jax.experimental import pallas as pl
from jax.experimental.pallas import tpu as pltpu
from jax.sharding import PartitionSpec as P

D = 8192
R = 512
NX, NY, NZ = 4, 4, 8
ROWS = 32
LOCAL_ROWS = NX * NY * NZ * ROWS
COLS = 256
WIDE = 384
MESH = pl.DeviceIdType.MESH
F32, BF16 = jnp.float32, jnp.bfloat16
HIGH = lax.Precision.HIGHEST
MIB = 2**20


def place():
    tp = lax.axis_index("tp")
    return lax.axis_index("dp"), lax.axis_index("fsdp"), lax.rem(tp, NY), lax.div(tp, NY)


def x_peer(d):
    p = lax.rem(lax.axis_index("dp") + d, NX)
    return p, {"dp": p}


def y_peer(d):
    _, _, y, z = place()
    p = lax.rem(y + d, NY)
    return p, {"tp": z * NY + p}


def z_peer(d):
    _, _, y, z = place()
    p = lax.rem(z + d, NZ)
    return p, {"tp": p * NY + y}


def pair_peer(d):
    x, c, _, _ = place()
    p = lax.rem(x * 2 + c + d, 2 * NX)
    return p, {"dp": lax.div(p, 2), "fsdp": lax.rem(p, 2)}


SPANS = {"x": (x_peer, NX), "y": (y_peer, NY), "z": (z_peer, NZ), "pair": (pair_peer, 2 * NX)}


def peers(axis):
    find, n = SPANS[axis]
    return [find(d) for d in range(1, n)]


class Sender:
    def __init__(self, send, recv):
        self.send, self.recv, self.used = send, recv, 0

    def make(self, src, dst, device):
        k = self.used
        self.used += 1
        return pltpu.make_async_remote_copy(
            src_ref=src,
            dst_ref=dst,
            send_sem=self.send.at[k],
            recv_sem=self.recv.at[k],
            device_id=device,
            device_id_type=MESH,
        )

    def start(self, src, dst, device):
        copy = self.make(src, dst, device)
        copy.start()
        return copy


def settle(copies):
    for copy in copies:
        copy.wait()


def splat_rows(v, i):
    return jnp.broadcast_to(v[i:i+1,:], (8,128))

def diag_inverse(load):
    n=16
    sub=lax.broadcasted_iota(jnp.int32,(8,128),0)
    lane=lax.broadcasted_iota(jnp.int32,(8,128),1)
    G=[load(g) for g in range(n)]
    Y=[(lane==sub+8*g).astype(F32) for g in range(n)]
    out=[]
    for p in range(n):
        at=8*p
        C=[jnp.broadcast_to(G[p][:,at+k:at+k+1],(8,128)) for k in range(8)]
        c={(i,k): splat_rows(C[k],i) for k in range(8) for i in range(k,8)}
        r=[None]*8; l={}
        for j in range(8):
            piv=c[j,j]
            rr=lax.rsqrt(piv)
            rr=rr*(1.5-0.5*piv*rr*rr)
            r[j]=rr
            for i in range(j+1,8): l[i,j]=c[i,j]*rr
            for k in range(j+1,8):
                for i in range(k,8):
                    c[i,k]=c[i,k]-l[i,j]*l[k,j]
        us,ys=[],[]
        g0,y0=G[p],Y[p]
        done_y=jnp.zeros((8,128),F32)
        Lc=[]
        for j in range(8):
            col=C[j]
            for i in range(j): col=col-Lc[i]*l[j,i]
            col=col*r[j]
            Lc.append(col)
            u=splat_rows(g0,j)*r[j]
            yv=splat_rows(y0,j)*r[j]
            us.append(u); ys.append(yv)
            m=jnp.where(sub>j,col,0.0)
            g0=g0-m*u
            y0=y0-m*yv
            done_y=jnp.where(sub==j,yv,done_y)
        out.append(done_y)
        for g in range(p+1,n):
            Cg=[jnp.broadcast_to(G[g][:,at+k:at+k+1],(8,128)) for k in range(8)]
            L=[]
            gg,yy=G[g],Y[g]
            for j in range(8):
                col=Cg[j]
                for i in range(j): col=col-L[i]*l[j,i]
                col=col*r[j]; L.append(col)
                gg=gg-col*us[j]
                yy=yy-col*ys[j]
            G[g],Y[g]=gg,yy
    return out

def nt(a, b, precision=HIGH):
    return lax.dot_general(
        a, b, (((1,), (1,)), ((), ())), precision=precision, preferred_element_type=F32
    )


def nn(a, b):
    return jnp.dot(a, b, precision=HIGH, preferred_element_type=F32)

def inverse_factor(a, out, between):
    out[...] = jnp.zeros_like(out)

    def step(kb, _):
        between(kb)
        base = pl.multiple_of(kb * 128, 128)
        rows = diag_inverse(lambda g: a[pl.ds(base + 8 * g, 8), pl.ds(base, 128)])
        for g in range(16):
            out[pl.ds(base + 8 * g, 8), pl.ds(base, 128)] = rows[g]
        for s in range(4):

            @pl.when(kb == s)
            def _():
                lo, hi = s * 128, (s + 1) * 128
                block = out[lo:hi, lo:hi]
                if s > 0:
                    out[lo:hi, 0:lo] = nn(block, out[lo:hi, 0:lo])
                if s < 3:
                    panel = nt(a[hi:R, lo:hi], block)
                    a[hi:R, hi:R] = a[hi:R, hi:R] - nt(panel, panel)
                    out[hi:R, 0:hi] = out[hi:R, 0:hi] - nn(panel, out[lo:hi, 0:hi])

        return 0

    lax.fori_loop(0, 4, step, 0)


def front_kernel(
    momentum, gradient, basis, left, right_low, next_low, new_basis,
    mom, grad, low, base, part, rx1, ry1, za, zb, zh, zs, sx1, sy1, sz1, rx2, ry2, rz2, sx2, sy2, sz2,
    rx3, ry3, rz3, gsend, grecv, tpart, trecv, right, inverse, following, own, ry, mid, rz,
    load, send, recv,
):
    x, c, y, z = place()
    sender = Sender(send, recv)
    sibling = {"fsdp": 1 - c}
    px, py, pz, around = peers("x"), peers("y"), peers("z"), peers("pair")
    barrier = pltpu.get_barrier_semaphore()
    greeted = [dev for _, dev in px + py + pz + around]
    for dev in greeted:
        pl.semaphore_signal(barrier, inc=1, device_id=dev, device_id_type=MESH)

    order = [p for p, _ in px] + [x]
    loads = []
    for k, p in enumerate(order):
        rows = pl.ds(pl.multiple_of(p * 1024, 1024), 1024)
        one = pltpu.make_async_copy(momentum.at[0, rows, :], mom.at[p], load.at[2 * k])
        two = pltpu.make_async_copy(gradient.at[0, rows, :], grad.at[p], load.at[2 * k + 1])
        one.start()
        two.start()
        loads.append((one, two))
    base[c] = basis[...].astype(BF16)
    pl.semaphore_wait(barrier, len(greeted))
    basis_copy = sender.start(base.at[c], base.at[c], sibling)

    top, low16 = pl.ds(0, 16), pl.ds(16, 16)
    wide, narrow = pl.ds(0, WIDE), pl.ds(WIDE, R - WIDE)
    x1 = []
    for k, p in enumerate(order):
        for copy in loads[k]:
            copy.wait()
        low[p] = (mom[p] + grad[p].astype(F32)).astype(BF16)
        if k == 0:
            basis_copy.wait()
        for h in range(2):
            value = jnp.dot(low[p], base[h], preferred_element_type=F32).astype(BF16)
            part[p, :, :, :, h * 256 : (h + 1) * 256] = value.reshape(NY, NZ, ROWS, 256)
        if k < NX - 1:
            dev = px[k][1]
            x1.append(sender.start(part.at[p, :, :, top, wide], rx1.at[k], dev))

    def on_z(d):
        p = lax.rem(z + d + NZ, NZ)
        return p, {"tp": p * NY + y}

    y1 = [sender.start(part.at[:, p, :, low16, wide], ry1.at[k], dev) for k, (p, dev) in enumerate(py)]
    halves = (pl.ds(0, 2), pl.ds(2, 2))
    far, _ = on_z(4)
    z1 = []
    for k, d in enumerate((-1, 1)):
        third, _ = on_z(3 * d)
        z1.append(sender.start(part.at[:, :, third, :, narrow], za.at[k], on_z(d)[1]))
    for k, d in enumerate((-1, 1)):
        z1.append(sender.start(part.at[halves[k], :, far, :, narrow], zh.at[k], on_z(2 * d)[1]))
    zb1 = []
    for k, d in enumerate((-1, 1)):
        near, dev = on_z(d)
        zb1.append(sender.start(part.at[:, :, near, :, narrow], zb.at[k], dev))
    settle(z1)
    for k, d in enumerate((-1, 1)):
        second, dev = on_z(2 * d)
        for i in range(NX):
            total = part[i, :, second, :, WIDE:R].astype(F32) + za[k, i].astype(F32)
            if i // 2 == k:
                total = total + zh[k, i % 2].astype(F32)
            zs[k, i] = total.astype(BF16)
        zb1.append(sender.start(zs.at[k], zb.at[2 + k], dev))
    settle(x1)
    for i in range(NY):
        total = part[x, i, :, 0:16, 0:WIDE].astype(F32)
        for k in range(NX - 1):
            total = total + rx1[k, i].astype(F32)
        sx1[i] = total.astype(BF16)
    x2 = [sender.start(sx1.at[p], rx2.at[k], dev) for k, (p, dev) in enumerate(py)]
    settle(y1)
    for i in range(NX):
        total = part[i, y, :, 16:32, 0:WIDE].astype(F32)
        for k in range(NY - 1):
            total = total + ry1[k, i].astype(F32)
        sy1[i] = total.astype(BF16)
    y2 = [sender.start(sy1.at[p], ry2.at[k], dev) for k, (p, dev) in enumerate(px)]
    settle(zb1)
    for i in range(NX):
        total = part[i, :, z, :, WIDE:R].astype(F32)
        for k in range(4):
            total = total + zb[k, i].astype(F32)
        sz1[i] = total.astype(BF16)
    z2 = [sender.start(sz1.at[p], rz2.at[k], dev) for k, (p, dev) in enumerate(px)]

    settle(x2)
    total = sx1[y].astype(F32)
    for k in range(NY - 1):
        total = total + rx2[k].astype(F32)
    sx2[...] = total.astype(BF16)
    x3 = [sender.start(sx2.at[p], rx3.at[k], dev) for k, (p, dev) in enumerate(pz)]
    settle(y2)
    total = sy1[x].astype(F32)
    for k in range(NX - 1):
        total = total + ry2[k].astype(F32)
    sy2[...] = total.astype(BF16)
    y3 = [sender.start(sy2.at[p], ry3.at[k], dev) for k, (p, dev) in enumerate(pz)]
    settle(z2)
    total = sz1[x].astype(F32)
    for k in range(NX - 1):
        total = total + rz2[k].astype(F32)
    sz2[...] = total.astype(BF16)
    z3 = [sender.start(sz2.at[p], rz3.at[k], dev) for k, (p, dev) in enumerate(py)]

    settle(x3)
    total = sx2[z].astype(F32)
    for k in range(NZ - 1):
        total = total + rx3[k].astype(F32)
    left[x, y, z, 0:16, 0:WIDE] = (total / NX).astype(BF16)
    mine = left.at[x, y, z, top, wide]
    x4 = [sender.start(mine, mine, dev) for _, dev in pz]
    settle(y3)
    total = sy2[z].astype(F32)
    for k in range(NZ - 1):
        total = total + ry3[k].astype(F32)
    left[x, y, z, 16:32, 0:WIDE] = (total / NX).astype(BF16)
    mine = left.at[x, y, z, low16, wide]
    y4 = [sender.start(mine, mine, dev) for _, dev in pz]
    settle(z3)
    total = sz2[y].astype(F32)
    for k in range(NY - 1):
        total = total + rz3[k].astype(F32)
    left[x, y, z, :, WIDE:R] = (total / NX).astype(BF16)
    mine = left.at[x, y, z, :, narrow]
    z4 = [sender.start(mine, mine, dev) for _, dev in py]

    settle(z4)
    mine = left.at[x, :, z, :, narrow]
    z5 = [sender.start(mine, mine, dev) for _, dev in px]
    settle(x4)
    mine = left.at[x, y, :, top, wide]
    x5 = [sender.start(mine, mine, dev) for _, dev in py]
    settle(y4)
    mine = left.at[x, y, :, low16, wide]
    y5 = [sender.start(mine, mine, dev) for _, dev in px]

    settle(z5)
    mine = left.at[:, :, z, :, narrow]
    z6 = {d: sender.start(mine, mine, on_z(d)[1]) for d in (1, -1, 2, -2)}
    settle(x5)
    mine = left.at[x, :, :, top, wide]
    x6 = [sender.start(mine, mine, dev) for _, dev in px]
    settle(y5)
    mine = left.at[:, y, :, low16, wide]
    y6 = [sender.start(mine, mine, dev) for _, dev in py]
    z7 = []
    for k, d in enumerate((1, -1)):
        z6[2 * d].wait()
        source, _ = on_z(-2 * d)
        piece = left.at[:, :, source, :, narrow]
        z7.append(sender.start(piece, piece, on_z(d)[1]))
        piece = left.at[halves[k], :, source, :, narrow]
        z7.append(sender.start(piece, piece, on_z(2 * d)[1]))
    z6[1].wait()
    z6[-1].wait()
    settle(z7 + x6 + y6)

    gsend[...] = jnp.zeros_like(gsend)
    tpart[...] = jnp.zeros_like(tpart)

    def products(xi, _):
        block = left[xi].reshape(1024, R)
        over_rows = (((0,), (0,)), ((), ()))
        gsend[...] += lax.dot_general(block, block, over_rows, preferred_element_type=F32)
        value = lax.dot_general(low[xi], block, over_rows, preferred_element_type=F32)
        tpart[...] += value.reshape(tpart.shape)
        return 0

    lax.fori_loop(0, NX, products, 0)
    g1 = sender.start(gsend, grecv, sibling)
    t1 = [sender.start(tpart.at[p], trecv.at[k], dev) for k, (p, dev) in enumerate(around)]
    me = x * 2 + c
    mine = right.at[me]
    t2 = [sender.make(mine, mine, dev) for _, dev in around]
    g1.wait()
    gsend[...] = gsend[...] + grecv[...]

    def between(kb):
        @pl.when(kb == 2)
        def _():
            settle(t1)
            total = tpart[me]
            for k in range(2 * NX - 1):
                total = total + trecv[k]
            right[me] = total / NX
            for copy in t2:
                copy.start()

    inverse_factor(gsend, inverse, between)
    grecv[...] = inverse[...] - inverse[...].astype(BF16).astype(F32)
    settle(t2)

    mean = nt(right[...].reshape(COLS, R), inverse[...])
    right_low[...] = mean.astype(BF16)
    following[...] = mean
    own[...] = jnp.broadcast_to(jnp.sum(mean * mean, axis=0, keepdims=True), own.shape)
    y7 = [sender.start(own, ry.at[k], dev) for k, (_, dev) in enumerate(py)]

    def ortho(xi, _):
        block = left[xi].reshape(1024, R)
        high = inverse[...].astype(BF16)
        rest = grecv[...].astype(BF16)
        value = nt(block, high, None) + nt(block, rest, None)
        left[xi] = value.astype(BF16).reshape(NY, NZ, ROWS, R)
        return 0

    lax.fori_loop(0, NX // 2, ortho, 0)
    settle(y7)
    value = own[...]
    for k in range(NY - 1):
        value = value + ry[k]
    mid[...] = value
    z8 = [sender.start(mid, rz.at[k], dev) for k, (_, dev) in enumerate(pz)]
    lax.fori_loop(NX // 2, NX, ortho, 0)
    settle(z8)
    value = mid[...]
    for k in range(NZ - 1):
        value = value + rz[k]
    scale = 1.0 / jnp.sqrt(value[0:1] / D + 1e-05)
    following[...] = following[...] * scale
    next_low[...] = following[...].astype(BF16)
    for core in range(2):

        @pl.when(c == core)
        def _():
            new_basis[...] = following[:, core * 256 : (core + 1) * 256]


def front(momentum, gradient, basis):
    vmem = pl.BlockSpec(memory_space=pltpu.VMEM)
    scratch = [
        pltpu.VMEM((NX, 1024, COLS), F32),
        pltpu.VMEM((NX, 1024, COLS), BF16),
        pltpu.VMEM((NX, 1024, COLS), BF16),
        pltpu.VMEM((2, COLS, 256), BF16),
        pltpu.VMEM((NX, NY, NZ, ROWS, R), BF16),
        pltpu.VMEM((3, NY, NZ, 16, WIDE), BF16),
        pltpu.VMEM((3, NX, NZ, 16, WIDE), BF16),
        pltpu.VMEM((2, NX, NY, ROWS, R - WIDE), BF16),
        pltpu.VMEM((4, NX, NY, ROWS, R - WIDE), BF16),
        pltpu.VMEM((2, 2, NY, ROWS, R - WIDE), BF16),
        pltpu.VMEM((2, NX, NY, ROWS, R - WIDE), BF16),
        pltpu.VMEM((NY, NZ, 16, WIDE), BF16),
        pltpu.VMEM((NX, NZ, 16, WIDE), BF16),
        pltpu.VMEM((NX, NY, ROWS, R - WIDE), BF16),
        pltpu.VMEM((3, NZ, 16, WIDE), BF16),
        pltpu.VMEM((3, NZ, 16, WIDE), BF16),
        pltpu.VMEM((3, NY, ROWS, R - WIDE), BF16),
        pltpu.VMEM((NZ, 16, WIDE), BF16),
        pltpu.VMEM((NZ, 16, WIDE), BF16),
        pltpu.VMEM((NY, ROWS, R - WIDE), BF16),
        pltpu.VMEM((7, 16, WIDE), BF16),
        pltpu.VMEM((7, 16, WIDE), BF16),
        pltpu.VMEM((3, ROWS, R - WIDE), BF16),
        pltpu.VMEM((R, R), F32),
        pltpu.VMEM((R, R), F32),
        pltpu.VMEM((8, 32, R), F32),
        pltpu.VMEM((7, 32, R), F32),
        pltpu.VMEM((8, 32, R), F32),
        pltpu.VMEM((R, R), F32),
        pltpu.VMEM((COLS, R), F32),
        pltpu.VMEM((8, R), F32),
        pltpu.VMEM((3, 8, R), F32),
        pltpu.VMEM((8, R), F32),
        pltpu.VMEM((7, 8, R), F32),
        pltpu.SemaphoreType.DMA((8,)),
        pltpu.SemaphoreType.DMA((112,)),
        pltpu.SemaphoreType.DMA((112,)),
    ]
    return pl.pallas_call(
        front_kernel,
        out_shape=(
            jax.ShapeDtypeStruct((NX, NY, NZ, ROWS, R), BF16),
            jax.ShapeDtypeStruct((COLS, R), BF16),
            jax.ShapeDtypeStruct((COLS, R), BF16),
            jax.ShapeDtypeStruct((COLS, 256), F32),
        ),
        in_specs=[pl.BlockSpec(memory_space=pl.ANY)] * 2 + [vmem],
        out_specs=(vmem,) * 4,
        scratch_shapes=scratch,
        compiler_params=pltpu.CompilerParams(
            collective_id=0, has_side_effects=True, vmem_limit_bytes=60 * MIB
        ),
        name="front",
    )(momentum, gradient, basis)


def finish_kernel(left, right, following, mom, grad, new_mom, update):
    ortho = left[...]
    across = (((1,), (1,)), ((), ()))
    lowrank = lax.dot_general(ortho, right[...], across, preferred_element_type=F32)
    new_mom[0] = mom[0] + grad[0].astype(F32) - 0.05 * lowrank
    factor = D / (R**0.5)
    product = lax.dot_general(ortho, following[...], across, preferred_element_type=F32)
    update[...] = (product * factor).astype(BF16)


def finish(left, right, following, momentum, gradient):
    tile = 512
    whole = lambda shape: pl.BlockSpec(shape, lambda i: (0,) * len(shape))
    rows = pl.BlockSpec((tile, R), lambda i: (i, 0))
    cube = pl.BlockSpec((1, tile, COLS), lambda i: (0, i, 0))
    return pl.pallas_call(
        finish_kernel,
        grid=(LOCAL_ROWS // tile,),
        out_shape=(
            jax.ShapeDtypeStruct((1, LOCAL_ROWS, COLS), F32),
            jax.ShapeDtypeStruct((LOCAL_ROWS, COLS), BF16),
        ),
        in_specs=[rows, whole((COLS, R)), whole((COLS, R)), cube, cube],
        out_specs=(cube, pl.BlockSpec((tile, COLS), lambda i: (i, 0))),
        compiler_params=pltpu.CompilerParams(vmem_limit_bytes=60 * MIB),
        name="finish",
    )(left, right, following, momentum, gradient)


def shards(momentum, gradient, basis):
    ortho, right, following, new_basis = front(momentum, gradient, basis)
    new_momentum, update = finish(
        ortho.reshape(LOCAL_ROWS, R), right, following, momentum, gradient
    )
    return (new_momentum, new_basis, update)


def solution(mesh):
    in_specs = (P("dp", "fsdp", "tp"), P("dp", "fsdp", "tp"), P("tp", "fsdp"))
    out_specs = (P("dp", "fsdp", "tp"), P("tp", "fsdp"), P("fsdp", "tp"))
    return jax.shard_map(shards, mesh=mesh, in_specs=in_specs, out_specs=out_specs, check_vma=False)
```

```python
import jax
import jax.numpy as jnp
from jax import lax
from jax.experimental import pallas as pl
from jax.experimental.pallas import tpu as pltpu
from jax.sharding import PartitionSpec as P

D = 8192
R = 512
NX, NY, NZ = 4, 4, 8
ROWS = 32
LOCAL_ROWS = NX * NY * NZ * ROWS
COLS = 256
WIDE = 384
MESH = pl.DeviceIdType.MESH
F32, BF16 = jnp.float32, jnp.bfloat16
HIGH = lax.Precision.HIGHEST
MIB = 2**20


def place():
    tp = lax.axis_index("tp")
    return lax.axis_index("dp"), lax.axis_index("fsdp"), lax.rem(tp, NY), lax.div(tp, NY)


def x_peer(d):
    p = lax.rem(lax.axis_index("dp") + d, NX)
    return p, {"dp": p}


def y_peer(d):
    _, _, y, z = place()
    p = lax.rem(y + d, NY)
    return p, {"tp": z * NY + p}


def z_peer(d):
    _, _, y, z = place()
    p = lax.rem(z + d, NZ)
    return p, {"tp": p * NY + y}


def pair_peer(d):
    x, c, _, _ = place()
    p = lax.rem(x * 2 + c + d, 2 * NX)
    return p, {"dp": lax.div(p, 2), "fsdp": lax.rem(p, 2)}


SPANS = {"x": (x_peer, NX), "y": (y_peer, NY), "z": (z_peer, NZ), "pair": (pair_peer, 2 * NX)}


def peers(axis):
    find, n = SPANS[axis]
    return [find(d) for d in range(1, n)]


class Sender:
    def __init__(self, send, recv):
        self.send, self.recv, self.used = send, recv, 0

    def make(self, src, dst, device):
        k = self.used
        self.used += 1
        return pltpu.make_async_remote_copy(
            src_ref=src,
            dst_ref=dst,
            send_sem=self.send.at[k],
            recv_sem=self.recv.at[k],
            device_id=device,
            device_id_type=MESH,
        )

    def start(self, src, dst, device):
        copy = self.make(src, dst, device)
        copy.start()
        return copy


def settle(copies):
    for copy in copies:
        copy.wait()


def splat_rows(v, i):
    return jnp.broadcast_to(v[i:i+1,:], (8,128))

def diag_inverse(load):
    n=16
    sub=lax.broadcasted_iota(jnp.int32,(8,128),0)
    lane=lax.broadcasted_iota(jnp.int32,(8,128),1)
    M=[load(g) for g in range(n)]
    out=[]
    for p in range(n):
        at=8*p
        inside=(lane>=at)&(lane<at+8)
        ident=(lane==sub+at).astype(F32)
        C=[jnp.broadcast_to(M[p][:,at+k:at+k+1],(8,128)) for k in range(8)]
        c={(i,k): splat_rows(C[k],i) for k in range(8) for i in range(k,8)}
        g0=jnp.where(inside,ident,M[p])
        grow=[splat_rows(g0,i) for i in range(8)]
        r=[None]*8; l={}
        us=[]
        done=jnp.zeros((8,128),F32)
        for j in range(8):
            rr=lax.rsqrt(c[j,j])
            r[j]=rr
            for i in range(j+1,8): l[i,j]=c[i,j]*rr
            for k in range(j+1,8):
                for i in range(k,8):
                    c[i,k]=c[i,k]-l[i,j]*l[k,j]
            t=grow[j]
            for k in range(j): t=t-l[j,k]*us[k]
            u=t*rr
            us.append(u)
            done=jnp.where(sub==j,u,done)
        out.append(done)
        def by_columns(g):
            Cg=[jnp.broadcast_to(M[g][:,at+k:at+k+1],(8,128)) for k in range(8)]
            L=[]
            gg=jnp.where(inside,0.0,M[g])
            for j in range(8):
                col=Cg[j]
                for i in range(j): col=col-L[i]*l[j,i]
                col=col*r[j]; L.append(col)
                gg=gg-col*us[j]
            M[g]=gg
        for g in range(p+1,n):
            by_columns(g)
    return [jnp.where(lane<=sub+8*g,out[g],0.0) for g in range(n)]


def nt(a, b, precision=HIGH):
    return lax.dot_general(
        a, b, (((1,), (1,)), ((), ())), precision=precision, preferred_element_type=F32
    )


def nn(a, b):
    return jnp.dot(a, b, precision=HIGH, preferred_element_type=F32)

def inverse_factor(a, out, between):
    out[...] = jnp.zeros_like(out)

    def step(kb, _):
        between(kb)
        base = pl.multiple_of(kb * 128, 128)
        rows = diag_inverse(lambda g: a[pl.ds(base + 8 * g, 8), pl.ds(base, 128)])
        for g in range(16):
            out[pl.ds(base + 8 * g, 8), pl.ds(base, 128)] = rows[g]
        for s in range(4):

            @pl.when(kb == s)
            def _():
                lo, hi = s * 128, (s + 1) * 128
                block = out[lo:hi, lo:hi]
                if s > 0:
                    out[lo:hi, 0:lo] = nn(block, out[lo:hi, 0:lo])
                if s < 3:
                    panel = nt(a[hi:R, lo:hi], block)
                    a[hi:R, hi:R] = a[hi:R, hi:R] - nt(panel, panel)
                    out[hi:R, 0:hi] = out[hi:R, 0:hi] - nn(panel, out[lo:hi, 0:hi])

        return 0

    lax.fori_loop(0, 4, step, 0)


def front_kernel(
    momentum, gradient, basis, ortho_out, right_low, next_low, new_basis,
    left, mom, grad, low, base, part, rx1, ry1, za, zb, zh, zs, sx1, sy1, sz1, rx2, ry2, rz2, sx2, sy2, sz2,
    rx3, ry3, rz3, gsend, grecv, tpart, trecv, right, inverse, following, own, ry, mid, rz,
    load, store, send, recv,
):
    x, c, y, z = place()
    sender = Sender(send, recv)
    sibling = {"fsdp": 1 - c}
    px, py, pz, around = peers("x"), peers("y"), peers("z"), peers("pair")
    barrier = pltpu.get_barrier_semaphore()
    greeted = [dev for _, dev in px + py + pz + around]
    for dev in greeted:
        pl.semaphore_signal(barrier, inc=1, device_id=dev, device_id_type=MESH)

    order = [p for p, _ in px] + [x]
    loads = []
    for k, p in enumerate(order):
        rows = pl.ds(pl.multiple_of(p * 1024, 1024), 1024)
        one = pltpu.make_async_copy(momentum.at[0, rows, :], mom.at[p], load.at[2 * k])
        two = pltpu.make_async_copy(gradient.at[0, rows, :], grad.at[p], load.at[2 * k + 1])
        one.start()
        two.start()
        loads.append((one, two))
    base[c] = basis[...].astype(BF16)

    def product(p, h):
        value = jnp.dot(low[p], base[h], preferred_element_type=F32).astype(BF16)
        columns = pl.ds(pl.multiple_of(h * 256, 256), 256)
        part[p, :, :, :, columns] = value.reshape(NY, NZ, ROWS, 256)

    for k, p in enumerate(order):
        for copy in loads[k]:
            copy.wait()
        low[p] = (mom[p] + grad[p].astype(F32)).astype(BF16)
        product(p, c)
    pl.semaphore_wait(barrier, len(greeted))
    basis_copy = sender.start(base.at[c], base.at[c], sibling)

    top, low16 = pl.ds(0, 16), pl.ds(16, 16)
    wide, narrow = pl.ds(0, WIDE), pl.ds(WIDE, R - WIDE)
    x1 = []
    basis_copy.wait()
    for k, p in enumerate(order):
        product(p, 1 - c)
        if k < NX - 1:
            dev = px[k][1]
            x1.append(sender.start(part.at[p, :, :, top, wide], rx1.at[k], dev))

    def on_z(d):
        p = lax.rem(z + d + NZ, NZ)
        return p, {"tp": p * NY + y}

    y1 = [sender.start(part.at[:, p, :, low16, wide], ry1.at[k], dev) for k, (p, dev) in enumerate(py)]
    halves = (pl.ds(0, 2), pl.ds(2, 2))
    far, _ = on_z(4)
    z1 = []
    for k, d in enumerate((-1, 1)):
        third, _ = on_z(3 * d)
        z1.append(sender.start(part.at[:, :, third, :, narrow], za.at[k], on_z(d)[1]))
    for k, d in enumerate((-1, 1)):
        z1.append(sender.start(part.at[halves[k], :, far, :, narrow], zh.at[k], on_z(2 * d)[1]))
    zb1 = []
    for k, d in enumerate((-1, 1)):
        near, dev = on_z(d)
        zb1.append(sender.start(part.at[:, :, near, :, narrow], zb.at[k], dev))
    settle(z1)
    for k, d in enumerate((-1, 1)):
        second, dev = on_z(2 * d)
        for i in range(NX):
            total = part[i, :, second, :, WIDE:R].astype(F32) + za[k, i].astype(F32)
            if i // 2 == k:
                total = total + zh[k, i % 2].astype(F32)
            zs[k, i] = total.astype(BF16)
        zb1.append(sender.start(zs.at[k], zb.at[2 + k], dev))
    settle(x1)
    for i in range(NY):
        total = part[x, i, :, 0:16, 0:WIDE].astype(F32)
        for k in range(NX - 1):
            total = total + rx1[k, i].astype(F32)
        sx1[i] = total.astype(BF16)
    x2 = [sender.start(sx1.at[p], rx2.at[k], dev) for k, (p, dev) in enumerate(py)]
    settle(y1)
    for i in range(NX):
        total = part[i, y, :, 16:32, 0:WIDE].astype(F32)
        for k in range(NY - 1):
            total = total + ry1[k, i].astype(F32)
        sy1[i] = total.astype(BF16)
    y2 = [sender.start(sy1.at[p], ry2.at[k], dev) for k, (p, dev) in enumerate(px)]
    settle(zb1)
    for i in range(NX):
        total = part[i, :, z, :, WIDE:R].astype(F32)
        for k in range(4):
            total = total + zb[k, i].astype(F32)
        sz1[i] = total.astype(BF16)
    z2 = [sender.start(sz1.at[p], rz2.at[k], dev) for k, (p, dev) in enumerate(px)]

    settle(x2)
    total = sx1[y].astype(F32)
    for k in range(NY - 1):
        total = total + rx2[k].astype(F32)
    sx2[...] = total.astype(BF16)
    x3 = [sender.start(sx2.at[p], rx3.at[k], dev) for k, (p, dev) in enumerate(pz)]
    settle(y2)
    total = sy1[x].astype(F32)
    for k in range(NX - 1):
        total = total + ry2[k].astype(F32)
    sy2[...] = total.astype(BF16)
    y3 = [sender.start(sy2.at[p], ry3.at[k], dev) for k, (p, dev) in enumerate(pz)]
    settle(z2)
    total = sz1[x].astype(F32)
    for k in range(NX - 1):
        total = total + rz2[k].astype(F32)
    sz2[...] = total.astype(BF16)
    z3 = [sender.start(sz2.at[p], rz3.at[k], dev) for k, (p, dev) in enumerate(py)]

    settle(x3)
    total = sx2[z].astype(F32)
    for k in range(NZ - 1):
        total = total + rx3[k].astype(F32)
    left[x, y, z, 0:16, 0:WIDE] = (total / NX).astype(BF16)
    mine = left.at[x, y, z, top, wide]
    x4 = [sender.start(mine, mine, dev) for _, dev in pz]
    settle(y3)
    total = sy2[z].astype(F32)
    for k in range(NZ - 1):
        total = total + ry3[k].astype(F32)
    left[x, y, z, 16:32, 0:WIDE] = (total / NX).astype(BF16)
    mine = left.at[x, y, z, low16, wide]
    y4 = [sender.start(mine, mine, dev) for _, dev in pz]
    settle(z3)
    total = sz2[y].astype(F32)
    for k in range(NY - 1):
        total = total + rz3[k].astype(F32)
    left[x, y, z, :, WIDE:R] = (total / NX).astype(BF16)
    mine = left.at[x, y, z, :, narrow]
    z4 = [sender.start(mine, mine, dev) for _, dev in py]

    settle(z4)
    mine = left.at[x, :, z, :, narrow]
    z5 = [sender.start(mine, mine, dev) for _, dev in px]
    settle(x4)
    mine = left.at[x, y, :, top, wide]
    x5 = [sender.start(mine, mine, dev) for _, dev in py]
    settle(y4)
    mine = left.at[x, y, :, low16, wide]
    y5 = [sender.start(mine, mine, dev) for _, dev in px]

    settle(z5)
    mine = left.at[:, :, z, :, narrow]
    z6 = {d: sender.start(mine, mine, on_z(d)[1]) for d in (1, -1, 2, -2)}
    settle(x5)
    mine = left.at[x, :, :, top, wide]
    x6 = [sender.start(mine, mine, dev) for _, dev in px]
    settle(y5)
    mine = left.at[:, y, :, low16, wide]
    y6 = [sender.start(mine, mine, dev) for _, dev in py]
    z7 = []
    for k, d in enumerate((1, -1)):
        z6[2 * d].wait()
        source, _ = on_z(-2 * d)
        piece = left.at[:, :, source, :, narrow]
        z7.append(sender.start(piece, piece, on_z(d)[1]))
        piece = left.at[halves[k], :, source, :, narrow]
        z7.append(sender.start(piece, piece, on_z(2 * d)[1]))
    z6[1].wait()
    z6[-1].wait()
    settle(z7 + x6 + y6)

    gsend[...] = jnp.zeros_like(gsend)
    tpart[...] = jnp.zeros_like(tpart)

    over_rows = (((0,), (0,)), ((), ()))

    def gram_of(xi, _):
        block = left[xi].reshape(1024, R)
        gsend[...] += lax.dot_general(block, block, over_rows, preferred_element_type=F32)
        return 0

    def right_of(xi, _):
        block = left[xi].reshape(1024, R)
        value = lax.dot_general(low[xi], block, over_rows, preferred_element_type=F32)
        tpart[...] += value.reshape(tpart.shape)
        return 0

    lax.fori_loop(0, NX, gram_of, 0)
    below, first = pl.ds(256, 256), pl.ds(0, 256)
    g1 = [
        sender.start(gsend.at[below, :], grecv.at[below, :], sibling),
        sender.start(gsend.at[first, first], grecv.at[first, first], sibling),
    ]
    lax.fori_loop(0, NX, right_of, 0)
    t1 = [sender.start(tpart.at[p], trecv.at[k], dev) for k, (p, dev) in enumerate(around)]
    me = x * 2 + c
    mine = right.at[me]
    t2 = [sender.make(mine, mine, dev) for _, dev in around]
    settle(g1)
    gsend[256:512, :] = gsend[256:512, :] + grecv[256:512, :]
    gsend[0:256, 0:256] = gsend[0:256, 0:256] + grecv[0:256, 0:256]

    def between(kb):
        @pl.when(kb == 2)
        def _():
            settle(t1)
            total = tpart[me]
            for k in range(2 * NX - 1):
                total = total + trecv[k]
            right[me] = total / NX
            for copy in t2:
                copy.start()

    inverse_factor(gsend, inverse, between)
    grecv[...] = inverse[...] - inverse[...].astype(BF16).astype(F32)
    settle(t2)

    mean = nt(right[...].reshape(COLS, R), inverse[...])
    right_low[...] = mean.astype(BF16)
    following[...] = mean
    own[...] = jnp.broadcast_to(jnp.sum(mean * mean, axis=0, keepdims=True), own.shape)
    y7 = [sender.start(own, ry.at[k], dev) for k, (_, dev) in enumerate(py)]

    def ortho(xi, _):
        block = left[xi].reshape(1024, R)
        high = inverse[...].astype(BF16)
        rest = grecv[...].astype(BF16)
        value = nt(block, high, None) + nt(block, rest, None)
        left[xi] = value.astype(BF16).reshape(NY, NZ, ROWS, R)
        pltpu.make_async_copy(left.at[xi], ortho_out.at[xi], store.at[xi]).start()
        return 0

    lax.fori_loop(0, NX // 2, ortho, 0)
    settle(y7)
    value = own[...]
    for k in range(NY - 1):
        value = value + ry[k]
    mid[...] = value
    z8 = [sender.start(mid, rz.at[k], dev) for k, (_, dev) in enumerate(pz)]
    lax.fori_loop(NX // 2, NX, ortho, 0)
    settle(z8)
    value = mid[...]
    for k in range(NZ - 1):
        value = value + rz[k]
    scale = 1.0 / jnp.sqrt(value[0:1] / D + 1e-05)
    following[...] = following[...] * scale
    next_low[...] = following[...].astype(BF16)
    for core in range(2):

        @pl.when(c == core)
        def _():
            new_basis[...] = following[:, core * 256 : (core + 1) * 256]

    for xi in range(NX):
        pltpu.make_async_copy(left.at[xi], ortho_out.at[xi], store.at[xi]).wait()


def front(momentum, gradient, basis):
    vmem = pl.BlockSpec(memory_space=pltpu.VMEM)
    scratch = [
        pltpu.VMEM((NX, NY, NZ, ROWS, R), BF16),
        pltpu.VMEM((NX, 1024, COLS), F32),
        pltpu.VMEM((NX, 1024, COLS), BF16),
        pltpu.VMEM((NX, 1024, COLS), BF16),
        pltpu.VMEM((2, COLS, 256), BF16),
        pltpu.VMEM((NX, NY, NZ, ROWS, R), BF16),
        pltpu.VMEM((3, NY, NZ, 16, WIDE), BF16),
        pltpu.VMEM((3, NX, NZ, 16, WIDE), BF16),
        pltpu.VMEM((2, NX, NY, ROWS, R - WIDE), BF16),
        pltpu.VMEM((4, NX, NY, ROWS, R - WIDE), BF16),
        pltpu.VMEM((2, 2, NY, ROWS, R - WIDE), BF16),
        pltpu.VMEM((2, NX, NY, ROWS, R - WIDE), BF16),
        pltpu.VMEM((NY, NZ, 16, WIDE), BF16),
        pltpu.VMEM((NX, NZ, 16, WIDE), BF16),
        pltpu.VMEM((NX, NY, ROWS, R - WIDE), BF16),
        pltpu.VMEM((3, NZ, 16, WIDE), BF16),
        pltpu.VMEM((3, NZ, 16, WIDE), BF16),
        pltpu.VMEM((3, NY, ROWS, R - WIDE), BF16),
        pltpu.VMEM((NZ, 16, WIDE), BF16),
        pltpu.VMEM((NZ, 16, WIDE), BF16),
        pltpu.VMEM((NY, ROWS, R - WIDE), BF16),
        pltpu.VMEM((7, 16, WIDE), BF16),
        pltpu.VMEM((7, 16, WIDE), BF16),
        pltpu.VMEM((3, ROWS, R - WIDE), BF16),
        pltpu.VMEM((R, R), F32),
        pltpu.VMEM((R, R), F32),
        pltpu.VMEM((8, 32, R), F32),
        pltpu.VMEM((7, 32, R), F32),
        pltpu.VMEM((8, 32, R), F32),
        pltpu.VMEM((R, R), F32),
        pltpu.VMEM((COLS, R), F32),
        pltpu.VMEM((8, R), F32),
        pltpu.VMEM((3, 8, R), F32),
        pltpu.VMEM((8, R), F32),
        pltpu.VMEM((7, 8, R), F32),
        pltpu.SemaphoreType.DMA((8,)),
        pltpu.SemaphoreType.DMA((NX,)),
        pltpu.SemaphoreType.DMA((112,)),
        pltpu.SemaphoreType.DMA((112,)),
    ]
    return pl.pallas_call(
        front_kernel,
        out_shape=(
            jax.ShapeDtypeStruct((NX, NY, NZ, ROWS, R), BF16),
            jax.ShapeDtypeStruct((COLS, R), BF16),
            jax.ShapeDtypeStruct((COLS, R), BF16),
            jax.ShapeDtypeStruct((COLS, 256), F32),
        ),
        in_specs=[pl.BlockSpec(memory_space=pl.ANY)] * 2 + [vmem],
        out_specs=(pl.BlockSpec(memory_space=pl.ANY),) + (vmem,) * 3,
        scratch_shapes=scratch,
        compiler_params=pltpu.CompilerParams(
            collective_id=0, has_side_effects=True, vmem_limit_bytes=60 * MIB
        ),
        name="front",
    )(momentum, gradient, basis)


def finish_kernel(left, right, following, mom, grad, new_mom, update):
    ortho = left[...]
    across = (((1,), (1,)), ((), ()))
    lowrank = lax.dot_general(ortho, right[...], across, preferred_element_type=F32)
    new_mom[0] = mom[0] + grad[0].astype(F32) - 0.05 * lowrank
    factor = D / (R**0.5)
    product = lax.dot_general(ortho, following[...], across, preferred_element_type=F32)
    update[...] = (product * factor).astype(BF16)


def finish(left, right, following, momentum, gradient):
    tile = 2048
    whole = lambda shape: pl.BlockSpec(shape, lambda i: (0,) * len(shape))
    rows = pl.BlockSpec((tile, R), lambda i: (i, 0))
    cube = pl.BlockSpec((1, tile, COLS), lambda i: (0, i, 0))
    return pl.pallas_call(
        finish_kernel,
        grid=(LOCAL_ROWS // tile,),
        out_shape=(
            jax.ShapeDtypeStruct((1, LOCAL_ROWS, COLS), F32),
            jax.ShapeDtypeStruct((LOCAL_ROWS, COLS), BF16),
        ),
        in_specs=[rows, whole((COLS, R)), whole((COLS, R)), cube, cube],
        out_specs=(cube, pl.BlockSpec((tile, COLS), lambda i: (i, 0))),
        compiler_params=pltpu.CompilerParams(vmem_limit_bytes=60 * MIB),
        name="finish",
    )(left, right, following, momentum, gradient)


def shards(momentum, gradient, basis):
    ortho, right, following, new_basis = front(momentum, gradient, basis)
    new_momentum, update = finish(
        ortho.reshape(LOCAL_ROWS, R), right, following, momentum, gradient
    )
    return (new_momentum, new_basis, update)


def solution(mesh):
    in_specs = (P("dp", "fsdp", "tp"), P("dp", "fsdp", "tp"), P("tp", "fsdp"))
    out_specs = (P("dp", "fsdp", "tp"), P("tp", "fsdp"), P("fsdp", "tp"))
    return jax.shard_map(shards, mesh=mesh, in_specs=in_specs, out_specs=out_specs, check_vma=False)
```

```python
import jax
import jax.numpy as jnp
from jax import lax
from jax.experimental import pallas as pl
from jax.experimental.pallas import tpu as pltpu
from jax.sharding import PartitionSpec as P

D = 8192
R = 512
NX, NY, NZ = 4, 4, 8
ROWS = 32
LOCAL_ROWS = NX * NY * NZ * ROWS
COLS = 256
WIDE = 384
MESH = pl.DeviceIdType.MESH
F32, BF16 = jnp.float32, jnp.bfloat16
HIGH = lax.Precision.HIGHEST
MIB = 2**20


def place():
    tp = lax.axis_index("tp")
    return lax.axis_index("dp"), lax.axis_index("fsdp"), lax.rem(tp, NY), lax.div(tp, NY)


def x_peer(d):
    p = lax.rem(lax.axis_index("dp") + d, NX)
    return p, {"dp": p}


def y_peer(d):
    _, _, y, z = place()
    p = lax.rem(y + d, NY)
    return p, {"tp": z * NY + p}


def z_peer(d):
    _, _, y, z = place()
    p = lax.rem(z + d, NZ)
    return p, {"tp": p * NY + y}


def pair_peer(d):
    x, c, _, _ = place()
    p = lax.rem(x * 2 + c + d, 2 * NX)
    return p, {"dp": lax.div(p, 2), "fsdp": lax.rem(p, 2)}


SPANS = {"x": (x_peer, NX), "y": (y_peer, NY), "z": (z_peer, NZ), "pair": (pair_peer, 2 * NX)}


def peers(axis):
    find, n = SPANS[axis]
    return [find(d) for d in range(1, n)]


class Sender:
    def __init__(self, send, recv):
        self.send, self.recv, self.used = send, recv, 0

    def make(self, src, dst, device):
        k = self.used
        self.used += 1
        return pltpu.make_async_remote_copy(
            src_ref=src,
            dst_ref=dst,
            send_sem=self.send.at[k],
            recv_sem=self.recv.at[k],
            device_id=device,
            device_id_type=MESH,
        )

    def start(self, src, dst, device):
        copy = self.make(src, dst, device)
        copy.start()
        return copy


def settle(copies):
    for copy in copies:
        copy.wait()


def splat_rows(v, i):
    return jnp.broadcast_to(v[i:i+1,:], (8,128))

def diag_inverse(load):
    n=16
    sub=lax.broadcasted_iota(jnp.int32,(8,128),0)
    lane=lax.broadcasted_iota(jnp.int32,(8,128),1)
    M=[load(g) for g in range(n)]
    out=[]
    for p in range(n):
        at=8*p
        inside=(lane>=at)&(lane<at+8)
        ident=(lane==sub+at).astype(F32)
        C=[jnp.broadcast_to(M[p][:,at+k:at+k+1],(8,128)) for k in range(8)]
        c={(i,k): splat_rows(C[k],i) for k in range(8) for i in range(k,8)}
        g0=jnp.where(inside,ident,M[p])
        grow=[splat_rows(g0,i) for i in range(8)]
        r=[None]*8; l={}
        us=[]
        done=jnp.zeros((8,128),F32)
        for j in range(8):
            rr=lax.rsqrt(c[j,j])
            r[j]=rr
            for i in range(j+1,8): l[i,j]=c[i,j]*rr
            for k in range(j+1,8):
                for i in range(k,8):
                    c[i,k]=c[i,k]-l[i,j]*l[k,j]
            t=grow[j]
            for k in range(j): t=t-l[j,k]*us[k]
            u=t*rr
            us.append(u)
            done=jnp.where(sub==j,u,done)
        out.append(done)
        def by_columns(g):
            Cg=[jnp.broadcast_to(M[g][:,at+k:at+k+1],(8,128)) for k in range(8)]
            L=[]
            gg=jnp.where(inside,0.0,M[g])
            for j in range(8):
                col=Cg[j]
                for i in range(j): col=col-L[i]*l[j,i]
                col=col*r[j]; L.append(col)
                gg=gg-col*us[j]
            M[g]=gg
        for g in range(p+1,n):
            by_columns(g)
    return [jnp.where(lane<=sub+8*g,out[g],0.0) for g in range(n)]


def nt(a, b, precision=HIGH):
    return lax.dot_general(
        a, b, (((1,), (1,)), ((), ())), precision=precision, preferred_element_type=F32
    )


def nn(a, b):
    return jnp.dot(a, b, precision=HIGH, preferred_element_type=F32)

def inverse_factor(a, out, between):
    out[...] = jnp.zeros_like(out)

    def step(kb, _):
        between(kb)
        base = pl.multiple_of(kb * 128, 128)
        rows = diag_inverse(lambda g: a[pl.ds(base + 8 * g, 8), pl.ds(base, 128)])
        for g in range(16):
            out[pl.ds(base + 8 * g, 8), pl.ds(base, 128)] = rows[g]
        for s in range(4):

            @pl.when(kb == s)
            def _():
                lo, hi = s * 128, (s + 1) * 128
                block = out[lo:hi, lo:hi]
                if s > 0:
                    out[lo:hi, 0:lo] = nn(block, out[lo:hi, 0:lo])
                if s < 3:
                    panel = nt(a[hi:R, lo:hi], block)
                    a[hi:R, hi:R] = a[hi:R, hi:R] - nt(panel, panel)
                    out[hi:R, 0:hi] = out[hi:R, 0:hi] - nn(panel, out[lo:hi, 0:hi])

        return 0

    lax.fori_loop(0, 4, step, 0)


def front_kernel(
    momentum, gradient, basis, ortho_out, right_low, next_low, new_basis,
    left, mom, grad, low, base, part, rx1, ry1, za, zb, zh, zs, sx1, sy1, sz1, rx2, ry2, rz2, sx2, sy2, sz2,
    rx3, ry3, rz3, gsend, grecv, tpart, trecv, right, inverse, halved, following, own, ry, mid, rz,
    load, store, send, recv,
):
    x, c, y, z = place()
    sender = Sender(send, recv)
    sibling = {"fsdp": 1 - c}
    px, py, pz, around = peers("x"), peers("y"), peers("z"), peers("pair")
    barrier = pltpu.get_barrier_semaphore()
    greeted = [dev for _, dev in px + py + pz + around]
    for dev in greeted:
        pl.semaphore_signal(barrier, inc=1, device_id=dev, device_id_type=MESH)

    order = [p for p, _ in px] + [x]
    loads = []
    for k, p in enumerate(order):
        rows = pl.ds(pl.multiple_of(p * 1024, 1024), 1024)
        one = pltpu.make_async_copy(momentum.at[0, rows, :], mom.at[p], load.at[2 * k])
        two = pltpu.make_async_copy(gradient.at[0, rows, :], grad.at[p], load.at[2 * k + 1])
        one.start()
        two.start()
        loads.append((one, two))
    base[c] = basis[...].astype(BF16)

    def product(p, h):
        value = jnp.dot(low[p], base[h], preferred_element_type=F32).astype(BF16)
        columns = pl.ds(pl.multiple_of(h * 256, 256), 256)
        part[p, :, :, :, columns] = value.reshape(NY, NZ, ROWS, 256)

    for k, p in enumerate(order):
        for copy in loads[k]:
            copy.wait()
        low[p] = (mom[p] + grad[p].astype(F32)).astype(BF16)
        product(p, c)
    pl.semaphore_wait(barrier, len(greeted))
    basis_copy = sender.start(base.at[c], base.at[c], sibling)

    top, low16 = pl.ds(0, 16), pl.ds(16, 16)
    wide, narrow = pl.ds(0, WIDE), pl.ds(WIDE, R - WIDE)
    x1 = []
    basis_copy.wait()
    for k, p in enumerate(order):
        product(p, 1 - c)
        if k < NX - 1:
            dev = px[k][1]
            x1.append(sender.start(part.at[p, :, :, top, wide], rx1.at[k], dev))

    def on_z(d):
        p = lax.rem(z + d + NZ, NZ)
        return p, {"tp": p * NY + y}

    y1 = [sender.start(part.at[:, p, :, low16, wide], ry1.at[k], dev) for k, (p, dev) in enumerate(py)]
    halves = (pl.ds(0, 2), pl.ds(2, 2))
    far, _ = on_z(4)
    z1 = []
    for k, d in enumerate((-1, 1)):
        third, _ = on_z(3 * d)
        z1.append(sender.start(part.at[:, :, third, :, narrow], za.at[k], on_z(d)[1]))
    for k, d in enumerate((-1, 1)):
        z1.append(sender.start(part.at[halves[k], :, far, :, narrow], zh.at[k], on_z(2 * d)[1]))
    zb1 = []
    for k, d in enumerate((-1, 1)):
        near, dev = on_z(d)
        zb1.append(sender.start(part.at[:, :, near, :, narrow], zb.at[k], dev))
    settle(z1)
    for k, d in enumerate((-1, 1)):
        second, dev = on_z(2 * d)
        for i in range(NX):
            total = part[i, :, second, :, WIDE:R].astype(F32) + za[k, i].astype(F32)
            if i // 2 == k:
                total = total + zh[k, i % 2].astype(F32)
            zs[k, i] = total.astype(BF16)
        zb1.append(sender.start(zs.at[k], zb.at[2 + k], dev))
    settle(x1)
    for i in range(NY):
        total = part[x, i, :, 0:16, 0:WIDE].astype(F32)
        for k in range(NX - 1):
            total = total + rx1[k, i].astype(F32)
        sx1[i] = total.astype(BF16)
    x2 = [sender.start(sx1.at[p], rx2.at[k], dev) for k, (p, dev) in enumerate(py)]
    settle(y1)
    for i in range(NX):
        total = part[i, y, :, 16:32, 0:WIDE].astype(F32)
        for k in range(NY - 1):
            total = total + ry1[k, i].astype(F32)
        sy1[i] = total.astype(BF16)
    y2 = [sender.start(sy1.at[p], ry2.at[k], dev) for k, (p, dev) in enumerate(px)]
    settle(zb1)
    for i in range(NX):
        total = part[i, :, z, :, WIDE:R].astype(F32)
        for k in range(4):
            total = total + zb[k, i].astype(F32)
        sz1[i] = total.astype(BF16)
    z2 = [sender.start(sz1.at[p], rz2.at[k], dev) for k, (p, dev) in enumerate(px)]

    settle(x2)
    total = sx1[y].astype(F32)
    for k in range(NY - 1):
        total = total + rx2[k].astype(F32)
    sx2[...] = total.astype(BF16)
    x3 = [sender.start(sx2.at[p], rx3.at[k], dev) for k, (p, dev) in enumerate(pz)]
    settle(y2)
    total = sy1[x].astype(F32)
    for k in range(NX - 1):
        total = total + ry2[k].astype(F32)
    sy2[...] = total.astype(BF16)
    y3 = [sender.start(sy2.at[p], ry3.at[k], dev) for k, (p, dev) in enumerate(pz)]
    settle(z2)
    total = sz1[x].astype(F32)
    for k in range(NX - 1):
        total = total + rz2[k].astype(F32)
    sz2[...] = total.astype(BF16)
    z3 = [sender.start(sz2.at[p], rz3.at[k], dev) for k, (p, dev) in enumerate(py)]

    settle(x3)
    total = sx2[z].astype(F32)
    for k in range(NZ - 1):
        total = total + rx3[k].astype(F32)
    left[x, y, z, 0:16, 0:WIDE] = (total / NX).astype(BF16)
    mine = left.at[x, y, z, top, wide]
    x4 = [sender.start(mine, mine, dev) for _, dev in pz]
    settle(y3)
    total = sy2[z].astype(F32)
    for k in range(NZ - 1):
        total = total + ry3[k].astype(F32)
    left[x, y, z, 16:32, 0:WIDE] = (total / NX).astype(BF16)
    mine = left.at[x, y, z, low16, wide]
    y4 = [sender.start(mine, mine, dev) for _, dev in pz]
    settle(z3)
    total = sz2[y].astype(F32)
    for k in range(NY - 1):
        total = total + rz3[k].astype(F32)
    left[x, y, z, :, WIDE:R] = (total / NX).astype(BF16)
    mine = left.at[x, y, z, :, narrow]
    z4 = [sender.start(mine, mine, dev) for _, dev in py]

    settle(z4)
    mine = left.at[x, :, z, :, narrow]
    z5 = [sender.start(mine, mine, dev) for _, dev in px]
    settle(x4)
    mine = left.at[x, y, :, top, wide]
    x5 = [sender.start(mine, mine, dev) for _, dev in py]
    settle(y4)
    mine = left.at[x, y, :, low16, wide]
    y5 = [sender.start(mine, mine, dev) for _, dev in px]

    settle(z5)
    mine = left.at[:, :, z, :, narrow]
    z6 = {d: sender.start(mine, mine, on_z(d)[1]) for d in (1, -1, 2, -2)}
    settle(x5)
    mine = left.at[x, :, :, top, wide]
    x6 = [sender.start(mine, mine, dev) for _, dev in px]
    settle(y5)
    mine = left.at[:, y, :, low16, wide]
    y6 = [sender.start(mine, mine, dev) for _, dev in py]
    z7 = []
    for k, d in enumerate((1, -1)):
        z6[2 * d].wait()
        source, _ = on_z(-2 * d)
        piece = left.at[:, :, source, :, narrow]
        z7.append(sender.start(piece, piece, on_z(d)[1]))
        piece = left.at[halves[k], :, source, :, narrow]
        z7.append(sender.start(piece, piece, on_z(2 * d)[1]))
    z6[1].wait()
    z6[-1].wait()
    settle(z7 + x6 + y6)

    gsend[...] = jnp.zeros_like(gsend)
    tpart[...] = jnp.zeros_like(tpart)

    over_rows = (((0,), (0,)), ((), ()))

    def gram_below(xi, _):
        block = left[xi].reshape(1024, R)
        gsend[256:512, :] += lax.dot_general(
            block[:, 256:512], block, over_rows, preferred_element_type=F32
        )
        return 0

    def gram_first(xi, _):
        block = left[xi, :, :, :, 0:256].reshape(1024, 256)
        gsend[0:256, 0:256] += lax.dot_general(
            block, block, over_rows, preferred_element_type=F32
        )
        return 0

    def right_of(xi, _):
        block = left[xi].reshape(1024, R)
        value = lax.dot_general(low[xi], block, over_rows, preferred_element_type=F32)
        tpart[...] += value.reshape(tpart.shape)
        return 0

    below, first = pl.ds(256, 256), pl.ds(0, 256)
    lax.fori_loop(0, NX, gram_below, 0)
    g1 = [sender.start(gsend.at[below, :], grecv.at[below, :], sibling)]
    lax.fori_loop(0, NX, gram_first, 0)
    g1.append(sender.start(gsend.at[first, first], grecv.at[first, first], sibling))
    lax.fori_loop(0, NX, right_of, 0)
    t1 = [sender.start(tpart.at[p], trecv.at[k], dev) for k, (p, dev) in enumerate(around)]
    me = x * 2 + c
    mine = right.at[me]
    t2 = [sender.make(mine, mine, dev) for _, dev in around]
    settle(g1)
    gsend[256:512, :] = gsend[256:512, :] + grecv[256:512, :]
    gsend[0:256, 0:256] = gsend[0:256, 0:256] + grecv[0:256, 0:256]

    def between(kb):
        @pl.when(kb == 2)
        def _():
            settle(t1)
            total = tpart[me]
            for k in range(2 * NX - 1):
                total = total + trecv[k]
            right[me] = total / NX
            for copy in t2:
                copy.start()

    inverse_factor(gsend, inverse, between)
    halved[0] = inverse[...].astype(BF16)
    halved[1] = (inverse[...] - inverse[...].astype(BF16).astype(F32)).astype(BF16)
    settle(t2)

    mean = nt(right[...].reshape(COLS, R), inverse[...])
    right_low[...] = mean.astype(BF16)
    following[...] = mean
    squares = jnp.sum(mean * mean, axis=0, keepdims=True)
    own[...] = jnp.zeros_like(own)
    for q in range(R // 128):
        own[q : q + 1, :] = squares[:, q * 128 : (q + 1) * 128]
    y7 = [sender.start(own, ry.at[k], dev) for k, (_, dev) in enumerate(py)]

    def ortho(xi, _):
        block = left[xi].reshape(1024, R)
        value = nt(block, halved[0], None) + nt(block, halved[1], None)
        left[xi] = value.astype(BF16).reshape(NY, NZ, ROWS, R)
        pltpu.make_async_copy(left.at[xi], ortho_out.at[xi], store.at[xi]).start()
        return 0

    lax.fori_loop(0, NX // 2, ortho, 0)
    settle(y7)
    value = own[...]
    for k in range(NY - 1):
        value = value + ry[k]
    mid[...] = value
    z8 = [sender.start(mid, rz.at[k], dev) for k, (_, dev) in enumerate(pz)]
    lax.fori_loop(NX // 2, NX, ortho, 0)
    settle(z8)
    value = mid[...]
    for k in range(NZ - 1):
        value = value + rz[k]
    squares = jnp.concatenate([value[q : q + 1] for q in range(R // 128)], axis=1)
    scale = 1.0 / jnp.sqrt(squares / D + 1e-05)
    following[...] = following[...] * scale
    next_low[...] = following[...].astype(BF16)
    for core in range(2):

        @pl.when(c == core)
        def _():
            new_basis[...] = following[:, core * 256 : (core + 1) * 256]

    for xi in range(NX):
        pltpu.make_async_copy(left.at[xi], ortho_out.at[xi], store.at[xi]).wait()


def front(momentum, gradient, basis):
    vmem = pl.BlockSpec(memory_space=pltpu.VMEM)
    scratch = [
        pltpu.VMEM((NX, NY, NZ, ROWS, R), BF16),
        pltpu.VMEM((NX, 1024, COLS), F32),
        pltpu.VMEM((NX, 1024, COLS), BF16),
        pltpu.VMEM((NX, 1024, COLS), BF16),
        pltpu.VMEM((2, COLS, 256), BF16),
        pltpu.VMEM((NX, NY, NZ, ROWS, R), BF16),
        pltpu.VMEM((3, NY, NZ, 16, WIDE), BF16),
        pltpu.VMEM((3, NX, NZ, 16, WIDE), BF16),
        pltpu.VMEM((2, NX, NY, ROWS, R - WIDE), BF16),
        pltpu.VMEM((4, NX, NY, ROWS, R - WIDE), BF16),
        pltpu.VMEM((2, 2, NY, ROWS, R - WIDE), BF16),
        pltpu.VMEM((2, NX, NY, ROWS, R - WIDE), BF16),
        pltpu.VMEM((NY, NZ, 16, WIDE), BF16),
        pltpu.VMEM((NX, NZ, 16, WIDE), BF16),
        pltpu.VMEM((NX, NY, ROWS, R - WIDE), BF16),
        pltpu.VMEM((3, NZ, 16, WIDE), BF16),
        pltpu.VMEM((3, NZ, 16, WIDE), BF16),
        pltpu.VMEM((3, NY, ROWS, R - WIDE), BF16),
        pltpu.VMEM((NZ, 16, WIDE), BF16),
        pltpu.VMEM((NZ, 16, WIDE), BF16),
        pltpu.VMEM((NY, ROWS, R - WIDE), BF16),
        pltpu.VMEM((7, 16, WIDE), BF16),
        pltpu.VMEM((7, 16, WIDE), BF16),
        pltpu.VMEM((3, ROWS, R - WIDE), BF16),
        pltpu.VMEM((R, R), F32),
        pltpu.VMEM((R, R), F32),
        pltpu.VMEM((8, 32, R), F32),
        pltpu.VMEM((7, 32, R), F32),
        pltpu.VMEM((8, 32, R), F32),
        pltpu.VMEM((R, R), F32),
        pltpu.VMEM((2, R, R), BF16),
        pltpu.VMEM((COLS, R), F32),
        pltpu.VMEM((8, 128), F32),
        pltpu.VMEM((3, 8, 128), F32),
        pltpu.VMEM((8, 128), F32),
        pltpu.VMEM((7, 8, 128), F32),
        pltpu.SemaphoreType.DMA((8,)),
        pltpu.SemaphoreType.DMA((NX,)),
        pltpu.SemaphoreType.DMA((112,)),
        pltpu.SemaphoreType.DMA((112,)),
    ]
    return pl.pallas_call(
        front_kernel,
        out_shape=(
            jax.ShapeDtypeStruct((NX, NY, NZ, ROWS, R), BF16),
            jax.ShapeDtypeStruct((COLS, R), BF16),
            jax.ShapeDtypeStruct((COLS, R), BF16),
            jax.ShapeDtypeStruct((COLS, 256), F32),
        ),
        in_specs=[pl.BlockSpec(memory_space=pl.ANY)] * 2 + [vmem],
        out_specs=(pl.BlockSpec(memory_space=pl.ANY),) + (vmem,) * 3,
        scratch_shapes=scratch,
        compiler_params=pltpu.CompilerParams(
            collective_id=0, has_side_effects=True, vmem_limit_bytes=60 * MIB
        ),
        name="front",
    )(momentum, gradient, basis)


def finish_kernel(left, right, following, basis, mom, grad, new_mom, new_basis, update):
    new_basis[...] = basis[...]
    ortho = left[...]
    across = (((1,), (1,)), ((), ()))
    lowrank = lax.dot_general(ortho, right[...], across, preferred_element_type=F32)
    new_mom[0] = mom[0] + grad[0].astype(F32) - 0.05 * lowrank
    factor = D / (R**0.5)
    product = lax.dot_general(ortho, following[...], across, preferred_element_type=F32)
    update[...] = (product * factor).astype(BF16)


def finish(left, right, following, basis, momentum, gradient):
    tile = 2048
    whole = lambda shape: pl.BlockSpec(shape, lambda i: (0,) * len(shape))
    rows = pl.BlockSpec((tile, R), lambda i: (i, 0))
    cube = pl.BlockSpec((1, tile, COLS), lambda i: (0, i, 0))
    return pl.pallas_call(
        finish_kernel,
        grid=(LOCAL_ROWS // tile,),
        out_shape=(
            jax.ShapeDtypeStruct((1, LOCAL_ROWS, COLS), F32),
            jax.ShapeDtypeStruct((COLS, 256), F32),
            jax.ShapeDtypeStruct((LOCAL_ROWS, COLS), BF16),
        ),
        in_specs=[rows, whole((COLS, R)), whole((COLS, R)), whole((COLS, 256)), cube, cube],
        out_specs=(cube, whole((COLS, 256)), pl.BlockSpec((tile, COLS), lambda i: (i, 0))),
        compiler_params=pltpu.CompilerParams(vmem_limit_bytes=60 * MIB),
        name="finish",
    )(left, right, following, basis, momentum, gradient)


def shards(momentum, gradient, basis):
    ortho, right, following, new_basis = front(momentum, gradient, basis)
    return finish(ortho.reshape(LOCAL_ROWS, R), right, following, new_basis, momentum, gradient)


def solution(mesh):
    in_specs = (P("dp", "fsdp", "tp"), P("dp", "fsdp", "tp"), P("tp", "fsdp"))
    out_specs = (P("dp", "fsdp", "tp"), P("tp", "fsdp"), P("fsdp", "tp"))
    return jax.shard_map(shards, mesh=mesh, in_specs=in_specs, out_specs=out_specs, check_vma=False)
```

```python
import jax
import jax.numpy as jnp
from jax import lax
from jax.experimental import pallas as pl
from jax.experimental.pallas import tpu as pltpu
from jax.sharding import PartitionSpec as P

D = 8192
R = 512
NX, NY, NZ = 4, 4, 8
ROWS = 32
LOCAL_ROWS = NX * NY * NZ * ROWS
COLS = 256
WIDE = 384
MESH = pl.DeviceIdType.MESH
F32, BF16 = jnp.float32, jnp.bfloat16
HIGH = lax.Precision.HIGHEST
MIB = 2**20


def place():
    tp = lax.axis_index("tp")
    return lax.axis_index("dp"), lax.axis_index("fsdp"), lax.rem(tp, NY), lax.div(tp, NY)


def x_peer(d):
    p = lax.rem(lax.axis_index("dp") + d, NX)
    return p, {"dp": p}


def y_peer(d):
    _, _, y, z = place()
    p = lax.rem(y + d, NY)
    return p, {"tp": z * NY + p}


def z_peer(d):
    _, _, y, z = place()
    p = lax.rem(z + d, NZ)
    return p, {"tp": p * NY + y}


def pair_peer(d):
    x, c, _, _ = place()
    p = lax.rem(x * 2 + c + d, 2 * NX)
    return p, {"dp": lax.div(p, 2), "fsdp": lax.rem(p, 2)}


SPANS = {"x": (x_peer, NX), "y": (y_peer, NY), "z": (z_peer, NZ), "pair": (pair_peer, 2 * NX)}


def peers(axis):
    find, n = SPANS[axis]
    return [find(d) for d in range(1, n)]


class Sender:
    def __init__(self, send, recv):
        self.send, self.recv, self.used = send, recv, 0

    def make(self, src, dst, device):
        k = self.used
        self.used += 1
        return pltpu.make_async_remote_copy(
            src_ref=src,
            dst_ref=dst,
            send_sem=self.send.at[k],
            recv_sem=self.recv.at[k],
            device_id=device,
            device_id_type=MESH,
        )

    def start(self, src, dst, device):
        copy = self.make(src, dst, device)
        copy.start()
        return copy


def settle(copies):
    for copy in copies:
        copy.wait()


def splat_rows(v, i):
    return jnp.broadcast_to(v[i:i+1,:], (8,128))

def diag_inverse(load):
    n=16
    sub=lax.broadcasted_iota(jnp.int32,(8,128),0)
    lane=lax.broadcasted_iota(jnp.int32,(8,128),1)
    M=[load(g) for g in range(n)]
    out=[]
    for p in range(n):
        at=8*p
        inside=(lane>=at)&(lane<at+8)
        ident=(lane==sub+at).astype(F32)
        C=[jnp.broadcast_to(M[p][:,at+k:at+k+1],(8,128)) for k in range(8)]
        c={(i,k): splat_rows(C[k],i) for k in range(8) for i in range(k,8)}
        g0=jnp.where(inside,ident,M[p])
        grow=[splat_rows(g0,i) for i in range(8)]
        r=[None]*8; l={}
        us=[]
        done=jnp.zeros((8,128),F32)
        for j in range(8):
            rr=lax.rsqrt(c[j,j])
            r[j]=rr
            for i in range(j+1,8): l[i,j]=c[i,j]*rr
            for k in range(j+1,8):
                for i in range(k,8):
                    c[i,k]=c[i,k]-l[i,j]*l[k,j]
            t=grow[j]
            for k in range(j): t=t-l[j,k]*us[k]
            u=t*rr
            us.append(u)
            done=jnp.where(sub==j,u,done)
        out.append(done)
        def by_columns(g):
            Cg=[jnp.broadcast_to(M[g][:,at+k:at+k+1],(8,128)) for k in range(8)]
            L=[]
            gg=jnp.where(inside,0.0,M[g])
            for j in range(8):
                col=Cg[j]
                for i in range(j): col=col-L[i]*l[j,i]
                col=col*r[j]; L.append(col)
                gg=gg-col*us[j]
            M[g]=gg
        for g in range(p+1,n):
            by_columns(g)
    return [jnp.where(lane<=sub+8*g,out[g],0.0) for g in range(n)]


def nt(a, b, precision=HIGH):
    return lax.dot_general(
        a, b, (((1,), (1,)), ((), ())), precision=precision, preferred_element_type=F32
    )


def nn(a, b):
    return jnp.dot(a, b, precision=HIGH, preferred_element_type=F32)

def inverse_factor(a, out, between):
    out[...] = jnp.zeros_like(out)

    def step(kb, _):
        between(kb)
        base = pl.multiple_of(kb * 128, 128)
        rows = diag_inverse(lambda g: a[pl.ds(base + 8 * g, 8), pl.ds(base, 128)])
        for g in range(16):
            out[pl.ds(base + 8 * g, 8), pl.ds(base, 128)] = rows[g]
        for s in range(4):

            @pl.when(kb == s)
            def _():
                lo, hi = s * 128, (s + 1) * 128
                block = out[lo:hi, lo:hi]
                if s > 0:
                    out[lo:hi, 0:lo] = nn(block, out[lo:hi, 0:lo])
                if s < 3:
                    panel = nt(a[hi:R, lo:hi], block)
                    a[hi:R, hi:R] = a[hi:R, hi:R] - nt(panel, panel)
                    out[hi:R, 0:hi] = out[hi:R, 0:hi] - nn(panel, out[lo:hi, 0:hi])

        return 0

    lax.fori_loop(0, 4, step, 0)


def front_kernel(
    momentum, gradient, basis, ortho_out, right_low, next_low, new_basis,
    left, mom, grad, low, base, part, rx1, ry1, za, zb, zh, zs, sx1, sy1, sz1, rx2, ry2, rz2, sx2, sy2, sz2,
    rx3, ry3, rz3, gsend, grecv, tpart, trecv, right, inverse, halved, following, own, ry, mid, rz,
    load, store, send, recv,
):
    x, c, y, z = place()
    sender = Sender(send, recv)
    sibling = {"fsdp": 1 - c}
    px, py, pz, around = peers("x"), peers("y"), peers("z"), peers("pair")
    barrier = pltpu.get_barrier_semaphore()
    greeted = [dev for _, dev in px + py + pz + around]
    for dev in greeted:
        pl.semaphore_signal(barrier, inc=1, device_id=dev, device_id_type=MESH)

    order = [p for p, _ in px] + [x]
    loads = []
    for k, p in enumerate(order):
        rows = pl.ds(pl.multiple_of(p * 1024, 1024), 1024)
        one = pltpu.make_async_copy(momentum.at[0, rows, :], mom.at[p], load.at[2 * k])
        two = pltpu.make_async_copy(gradient.at[0, rows, :], grad.at[p], load.at[2 * k + 1])
        one.start()
        two.start()
        loads.append((one, two))
    base[c] = basis[...].astype(BF16)

    def product(p, h):
        value = jnp.dot(low[p], base[h], preferred_element_type=F32).astype(BF16)
        columns = pl.ds(pl.multiple_of(h * 256, 256), 256)
        part[p, :, :, :, columns] = value.reshape(NY, NZ, ROWS, 256)

    for k, p in enumerate(order):
        for copy in loads[k]:
            copy.wait()
        low[p] = (mom[p] + grad[p].astype(F32)).astype(BF16)
        product(p, c)
    pl.semaphore_wait(barrier, len(greeted))
    basis_copy = sender.start(base.at[c], base.at[c], sibling)

    top, low16 = pl.ds(0, 16), pl.ds(16, 16)
    wide, narrow = pl.ds(0, WIDE), pl.ds(WIDE, R - WIDE)
    x1 = []
    basis_copy.wait()
    for k, p in enumerate(order):
        product(p, 1 - c)
        if k < NX - 1:
            dev = px[k][1]
            x1.append(sender.start(part.at[p, :, :, top, wide], rx1.at[k], dev))

    def on_z(d):
        p = lax.rem(z + d + NZ, NZ)
        return p, {"tp": p * NY + y}

    y1 = [sender.start(part.at[:, p, :, low16, wide], ry1.at[k], dev) for k, (p, dev) in enumerate(py)]
    halves = (pl.ds(0, 2), pl.ds(2, 2))
    far, _ = on_z(4)
    z1 = []
    for k, d in enumerate((-1, 1)):
        third, _ = on_z(3 * d)
        z1.append(sender.start(part.at[:, :, third, :, narrow], za.at[k], on_z(d)[1]))
    for k, d in enumerate((-1, 1)):
        z1.append(sender.start(part.at[halves[k], :, far, :, narrow], zh.at[k], on_z(2 * d)[1]))
    zb1 = []
    for k, d in enumerate((-1, 1)):
        near, dev = on_z(d)
        zb1.append(sender.start(part.at[:, :, near, :, narrow], zb.at[k], dev))
    settle(z1)
    for k, d in enumerate((-1, 1)):
        second, dev = on_z(2 * d)
        for i in range(NX):
            total = part[i, :, second, :, WIDE:R].astype(F32) + za[k, i].astype(F32)
            if i // 2 == k:
                total = total + zh[k, i % 2].astype(F32)
            zs[k, i] = total.astype(BF16)
        zb1.append(sender.start(zs.at[k], zb.at[2 + k], dev))
    settle(x1)
    for i in range(NY):
        total = part[x, i, :, 0:16, 0:WIDE].astype(F32)
        for k in range(NX - 1):
            total = total + rx1[k, i].astype(F32)
        sx1[i] = total.astype(BF16)
    x2 = [sender.start(sx1.at[p], rx2.at[k], dev) for k, (p, dev) in enumerate(py)]
    settle(y1)
    for i in range(NX):
        total = part[i, y, :, 16:32, 0:WIDE].astype(F32)
        for k in range(NY - 1):
            total = total + ry1[k, i].astype(F32)
        sy1[i] = total.astype(BF16)
    y2 = [sender.start(sy1.at[p], ry2.at[k], dev) for k, (p, dev) in enumerate(px)]
    settle(zb1)
    for i in range(NX):
        total = part[i, :, z, :, WIDE:R].astype(F32)
        for k in range(4):
            total = total + zb[k, i].astype(F32)
        sz1[i] = total.astype(BF16)
    z2 = [sender.start(sz1.at[p], rz2.at[k], dev) for k, (p, dev) in enumerate(px)]

    settle(x2)
    total = sx1[y].astype(F32)
    for k in range(NY - 1):
        total = total + rx2[k].astype(F32)
    sx2[...] = total.astype(BF16)
    x3 = [sender.start(sx2.at[p], rx3.at[k], dev) for k, (p, dev) in enumerate(pz)]
    settle(y2)
    total = sy1[x].astype(F32)
    for k in range(NX - 1):
        total = total + ry2[k].astype(F32)
    sy2[...] = total.astype(BF16)
    y3 = [sender.start(sy2.at[p], ry3.at[k], dev) for k, (p, dev) in enumerate(pz)]
    settle(z2)
    total = sz1[x].astype(F32)
    for k in range(NX - 1):
        total = total + rz2[k].astype(F32)
    sz2[...] = total.astype(BF16)
    z3 = [sender.start(sz2.at[p], rz3.at[k], dev) for k, (p, dev) in enumerate(py)]

    settle(x3)
    total = sx2[z].astype(F32)
    for k in range(NZ - 1):
        total = total + rx3[k].astype(F32)
    left[x, y, z, 0:16, 0:WIDE] = (total / NX).astype(BF16)
    mine = left.at[x, y, z, top, wide]
    x4 = [sender.start(mine, mine, dev) for _, dev in pz]
    settle(y3)
    total = sy2[z].astype(F32)
    for k in range(NZ - 1):
        total = total + ry3[k].astype(F32)
    left[x, y, z, 16:32, 0:WIDE] = (total / NX).astype(BF16)
    mine = left.at[x, y, z, low16, wide]
    y4 = [sender.start(mine, mine, dev) for _, dev in pz]
    settle(z3)
    total = sz2[y].astype(F32)
    for k in range(NY - 1):
        total = total + rz3[k].astype(F32)
    left[x, y, z, :, WIDE:R] = (total / NX).astype(BF16)
    mine = left.at[x, y, z, :, narrow]
    z4 = [sender.start(mine, mine, dev) for _, dev in py]

    settle(z4)
    mine = left.at[x, :, z, :, narrow]
    z5 = [sender.start(mine, mine, dev) for _, dev in px]
    settle(x4)
    mine = left.at[x, y, :, top, wide]
    x5 = [sender.start(mine, mine, dev) for _, dev in py]
    settle(y4)
    mine = left.at[x, y, :, low16, wide]
    y5 = [sender.start(mine, mine, dev) for _, dev in px]

    settle(z5)
    mine = left.at[:, :, z, :, narrow]
    z6 = {d: sender.start(mine, mine, on_z(d)[1]) for d in (1, -1, 2, -2)}
    settle(x5)
    mine = left.at[x, :, :, top, wide]
    x6 = [sender.start(mine, mine, dev) for _, dev in px]
    settle(y5)
    mine = left.at[:, y, :, low16, wide]
    y6 = [sender.start(mine, mine, dev) for _, dev in py]
    z7 = []
    for k, d in enumerate((1, -1)):
        z6[2 * d].wait()
        source, _ = on_z(-2 * d)
        piece = left.at[:, :, source, :, narrow]
        z7.append(sender.start(piece, piece, on_z(d)[1]))
        piece = left.at[halves[k], :, source, :, narrow]
        z7.append(sender.start(piece, piece, on_z(2 * d)[1]))
    z6[1].wait()
    z6[-1].wait()
    settle(z7 + x6 + y6)

    gsend[...] = jnp.zeros_like(gsend)
    tpart[...] = jnp.zeros_like(tpart)

    over_rows = (((0,), (0,)), ((), ()))

    def gram_below(xi, _):
        block = left[xi].reshape(1024, R)
        gsend[256:512, :] += lax.dot_general(
            block[:, 256:512], block, over_rows, preferred_element_type=F32
        )
        return 0

    def gram_first(xi, _):
        block = left[xi, :, :, :, 0:256].reshape(1024, 256)
        gsend[0:256, 0:256] += lax.dot_general(
            block, block, over_rows, preferred_element_type=F32
        )
        return 0

    def right_of(xi, _):
        block = left[xi].reshape(1024, R)
        value = lax.dot_general(low[xi], block, over_rows, preferred_element_type=F32)
        tpart[...] += value.reshape(tpart.shape)
        return 0

    below, first = pl.ds(256, 256), pl.ds(0, 256)
    lax.fori_loop(0, NX, gram_below, 0)
    g1 = [sender.start(gsend.at[below, :], grecv.at[below, :], sibling)]
    lax.fori_loop(0, NX, gram_first, 0)
    g1.append(sender.start(gsend.at[first, first], grecv.at[first, first], sibling))
    lax.fori_loop(0, NX, right_of, 0)
    t1 = [sender.start(tpart.at[p], trecv.at[k], dev) for k, (p, dev) in enumerate(around)]
    me = x * 2 + c
    mine = right.at[me]
    t2 = [sender.make(mine, mine, dev) for _, dev in around]
    settle(g1)
    gsend[256:512, :] = gsend[256:512, :] + grecv[256:512, :]
    gsend[0:256, 0:256] = gsend[0:256, 0:256] + grecv[0:256, 0:256]

    def between(kb):
        @pl.when(kb == 2)
        def _():
            settle(t1)
            total = tpart[me]
            for k in range(2 * NX - 1):
                total = total + trecv[k]
            right[me] = total / NX
            for copy in t2:
                copy.start()

    inverse_factor(gsend, inverse, between)
    halved[0] = inverse[...].astype(BF16)
    halved[1] = (inverse[...] - inverse[...].astype(BF16).astype(F32)).astype(BF16)
    settle(t2)

    mean = nt(right[...].reshape(COLS, R), inverse[...])
    right_low[...] = mean.astype(BF16)
    following[...] = mean
    squares = jnp.sum(mean * mean, axis=0, keepdims=True)
    own[...] = jnp.zeros_like(own)
    for q in range(R // 128):
        own[q : q + 1, :] = squares[:, q * 128 : (q + 1) * 128]
    y7 = [sender.start(own, ry.at[k], dev) for k, (_, dev) in enumerate(py)]

    def ortho(xi, _):
        block = left[xi].reshape(1024, R)
        value = nt(block, halved[0], None) + nt(block, halved[1], None)
        left[xi] = value.astype(BF16).reshape(NY, NZ, ROWS, R)
        pltpu.make_async_copy(left.at[xi], ortho_out.at[xi], store.at[xi]).start()
        return 0

    lax.fori_loop(0, NX // 2, ortho, 0)
    settle(y7)
    value = own[...]
    for k in range(NY - 1):
        value = value + ry[k]
    mid[...] = value
    z8 = [sender.start(mid, rz.at[k], dev) for k, (_, dev) in enumerate(pz)]
    lax.fori_loop(NX // 2, NX, ortho, 0)
    settle(z8)
    value = mid[...]
    for k in range(NZ - 1):
        value = value + rz[k]
    squares = jnp.concatenate([value[q : q + 1] for q in range(R // 128)], axis=1)
    scale = 1.0 / jnp.sqrt(squares / D + 1e-05)
    following[...] = following[...] * scale
    next_low[...] = following[...].astype(BF16)
    for core in range(2):

        @pl.when(c == core)
        def _():
            new_basis[...] = following[:, core * 256 : (core + 1) * 256]

    for xi in range(NX):
        pltpu.make_async_copy(left.at[xi], ortho_out.at[xi], store.at[xi]).wait()


def front(momentum, gradient, basis):
    vmem = pl.BlockSpec(memory_space=pltpu.VMEM)
    scratch = [
        pltpu.VMEM((NX, NY, NZ, ROWS, R), BF16),
        pltpu.VMEM((NX, 1024, COLS), F32),
        pltpu.VMEM((NX, 1024, COLS), BF16),
        pltpu.VMEM((NX, 1024, COLS), BF16),
        pltpu.VMEM((2, COLS, 256), BF16),
        pltpu.VMEM((NX, NY, NZ, ROWS, R), BF16),
        pltpu.VMEM((3, NY, NZ, 16, WIDE), BF16),
        pltpu.VMEM((3, NX, NZ, 16, WIDE), BF16),
        pltpu.VMEM((2, NX, NY, ROWS, R - WIDE), BF16),
        pltpu.VMEM((4, NX, NY, ROWS, R - WIDE), BF16),
        pltpu.VMEM((2, 2, NY, ROWS, R - WIDE), BF16),
        pltpu.VMEM((2, NX, NY, ROWS, R - WIDE), BF16),
        pltpu.VMEM((NY, NZ, 16, WIDE), BF16),
        pltpu.VMEM((NX, NZ, 16, WIDE), BF16),
        pltpu.VMEM((NX, NY, ROWS, R - WIDE), BF16),
        pltpu.VMEM((3, NZ, 16, WIDE), BF16),
        pltpu.VMEM((3, NZ, 16, WIDE), BF16),
        pltpu.VMEM((3, NY, ROWS, R - WIDE), BF16),
        pltpu.VMEM((NZ, 16, WIDE), BF16),
        pltpu.VMEM((NZ, 16, WIDE), BF16),
        pltpu.VMEM((NY, ROWS, R - WIDE), BF16),
        pltpu.VMEM((7, 16, WIDE), BF16),
        pltpu.VMEM((7, 16, WIDE), BF16),
        pltpu.VMEM((3, ROWS, R - WIDE), BF16),
        pltpu.VMEM((R, R), F32),
        pltpu.VMEM((R, R), F32),
        pltpu.VMEM((8, 32, R), F32),
        pltpu.VMEM((7, 32, R), F32),
        pltpu.VMEM((8, 32, R), F32),
        pltpu.VMEM((R, R), F32),
        pltpu.VMEM((2, R, R), BF16),
        pltpu.VMEM((COLS, R), F32),
        pltpu.VMEM((8, 128), F32),
        pltpu.VMEM((3, 8, 128), F32),
        pltpu.VMEM((8, 128), F32),
        pltpu.VMEM((7, 8, 128), F32),
        pltpu.SemaphoreType.DMA((8,)),
        pltpu.SemaphoreType.DMA((NX,)),
        pltpu.SemaphoreType.DMA((112,)),
        pltpu.SemaphoreType.DMA((112,)),
    ]
    return pl.pallas_call(
        front_kernel,
        out_shape=(
            jax.ShapeDtypeStruct((NX, NY, NZ, ROWS, R), BF16),
            jax.ShapeDtypeStruct((COLS, R), BF16),
            jax.ShapeDtypeStruct((COLS, R), BF16),
            jax.ShapeDtypeStruct((COLS, 256), F32),
        ),
        in_specs=[pl.BlockSpec(memory_space=pl.ANY)] * 2 + [vmem],
        out_specs=(pl.BlockSpec(memory_space=pl.ANY),) + (vmem,) * 3,
        scratch_shapes=scratch,
        compiler_params=pltpu.CompilerParams(
            collective_id=0, has_side_effects=True, vmem_limit_bytes=40 * MIB
        ),
        name="front",
    )(momentum, gradient, basis)


def finish_kernel(left, right, following, basis, mom, grad, new_mom, new_basis, update):
    new_basis[...] = basis[...]
    ortho = left[...]
    across = (((1,), (1,)), ((), ()))
    lowrank = lax.dot_general(ortho, right[...], across, preferred_element_type=F32)
    new_mom[0] = mom[0] + grad[0].astype(F32) - 0.05 * lowrank
    factor = D / (R**0.5)
    product = lax.dot_general(ortho, following[...], across, preferred_element_type=F32)
    update[...] = (product * factor).astype(BF16)


def finish(left, right, following, basis, momentum, gradient):
    tile = 2048
    whole = lambda shape: pl.BlockSpec(shape, lambda i: (0,) * len(shape))
    rows = pl.BlockSpec((tile, R), lambda i: (i, 0))
    cube = pl.BlockSpec((1, tile, COLS), lambda i: (0, i, 0))
    return pl.pallas_call(
        finish_kernel,
        grid=(LOCAL_ROWS // tile,),
        out_shape=(
            jax.ShapeDtypeStruct((1, LOCAL_ROWS, COLS), F32),
            jax.ShapeDtypeStruct((COLS, 256), F32),
            jax.ShapeDtypeStruct((LOCAL_ROWS, COLS), BF16),
        ),
        in_specs=[rows, whole((COLS, R)), whole((COLS, R)), whole((COLS, 256)), cube, cube],
        out_specs=(cube, whole((COLS, 256)), pl.BlockSpec((tile, COLS), lambda i: (i, 0))),
        compiler_params=pltpu.CompilerParams(vmem_limit_bytes=24 * MIB),
        name="finish",
    )(left, right, following, basis, momentum, gradient)


def shards(momentum, gradient, basis):
    ortho, right, following, new_basis = front(momentum, gradient, basis)
    return finish(ortho.reshape(LOCAL_ROWS, R), right, following, new_basis, momentum, gradient)


def solution(mesh):
    in_specs = (P("dp", "fsdp", "tp"), P("dp", "fsdp", "tp"), P("tp", "fsdp"))
    out_specs = (P("dp", "fsdp", "tp"), P("tp", "fsdp"), P("fsdp", "tp"))
    return jax.shard_map(shards, mesh=mesh, in_specs=in_specs, out_specs=out_specs, check_vma=False)
```
